256 devices in a mesh: replica: 32 (over y, z_lo, core), fsdp: 8 (over z_hi, x).
Axes of the slice: x: 4, y: 4, z: 8 (z_hi: 2, z_lo: 4; z = z_hi * 4 + z_lo), core: 2. Of those that a mesh axis runs over, the one named last changes fastest.
Arguments:
- params: bfloat16 [32, 4608, 1024], P('replica', 'fsdp'), may hold values from -6 to 6
- tokens: bfloat16 [32, 4096, 4608], P('replica', 'fsdp'), may hold values from -6 to 6
- cotangent: bfloat16 [32, 4096, 1024], P('replica', 'fsdp'), may hold values from -0.1875 to 0.1875
- gain: float32 [4608], replicated, may hold values from 0.1 to 1.9
- glob: float32 [4608, 1024], P(('fsdp', 'replica')), may hold values from -6 to 6
- momentum: float32 [4608, 1024], P(('fsdp', 'replica')), may hold values from -4 to 4
- prev_global: float32 [4608, 1024], P(('fsdp', 'replica')), may hold values from -6 to 6
Outputs:
- new_params: bfloat16 [32, 4608, 1024], P('replica', 'fsdp')
- grad_tokens: bfloat16 [32, 4096, 4608], P('replica', 'fsdp')
- new_global: float32 [4608, 1024], P(('fsdp', 'replica'))
- new_momentum: float32 [4608, 1024], P(('fsdp', 'replica'))
The draws below stay inside these ranges and needn't reach their ends.
All inputs are finite; a program needn't handle non-finite values.
Results may differ from the reference program's by a relative error of at most 0.014.
Values may be sent and summed in bfloat16 or wider, within the bound.
A program may use at most 128 MiB of HBM per device.

```python
import jax
import jax.numpy as jnp
from jax import lax

D = 4608
HV = 1024
TOK_DEV = 512
REPLICAS = 32
TOK_REP = 4096
N_FSDP = 8


def with_spikes(drawn, stream_key, source, target, shards_of, factor):
    def block_of(position):
        return (jnp.arange(drawn.shape[position]) // (drawn.shape[position] // shards_of)).reshape((-1,) + (1,) * (drawn.ndim - 1 - position))

    first = jax.random.permutation(stream_key, shards_of)[block_of(target)]
    far = (block_of(target) + shards_of // 2) % shards_of
    return jnp.where((block_of(source) == first) | (block_of(source) == far), factor * drawn, drawn)


def levels(stream_key, dims, pieces, least, largest):
    loudness = 1.0
    for dim, blocks in pieces:
        heights = jax.random.uniform(jax.random.fold_in(jax.random.fold_in(stream_key, 6), dim), (blocks,), jnp.float32, least / len(pieces), largest / len(pieces))
        loudness = loudness * jnp.repeat(jnp.exp(heights), dims[dim] // blocks).reshape((-1,) + (1,) * (len(dims) - 1 - dim))
    return loudness


def noise(key, extent, width, bound, pieces=(), held_as=jnp.bfloat16):
    loudness = levels(key, extent, pieces, -0.22, 0.18) if pieces else 1.0
    values = jax.random.normal(key, extent, jnp.float32) * width * loudness
    return jnp.minimum(jnp.maximum(values, -bound), bound).astype(held_as)


def bell_draw_with(stream_key, shape, spread, reach, split, heavy, dtype=jnp.bfloat16):
    entries = spread * jax.random.normal(stream_key, shape, jnp.float32)
    if split:
        entries = entries * levels(stream_key, shape, split, -0.22, 0.18)
    return jnp.clip(with_spikes(entries, jax.random.fold_in(stream_key, 3), *heavy), -reach, reach).astype(dtype)


def setup_inputs(seed: int = 0) -> dict:
    splits = jax.random.split(jax.random.key(seed), 8)
    params = bell_draw_with(splits[0], (REPLICAS, D, HV), 1.0, 6.0, ((0, 32), (1, 8)), (0, 1, 32, 2.75))
    tokens = noise(splits[1], (REPLICAS, TOK_REP, D), 1.0, 6.0, ((0, 32), (1, 8)))
    cotangent = noise(splits[2], (REPLICAS, TOK_REP, HV), HV ** -0.5, 0.1875, ((0, 32), (1, 8)))
    gain = jnp.clip(1.0 + 0.18 * jax.random.normal(splits[3], (D,), jnp.float32), 0.1, 1.9)
    glob = noise(splits[4], (D, HV), 1.0, 6.0, ((0, 256),), jnp.float32)
    momentum = noise(splits[5], (D, HV), 0.3, 4.0, ((0, 256),), jnp.float32)
    prev_global = noise(splits[6], (D, HV), 1.0, 6.0, ((0, 256),), jnp.float32)
    return {"params": params, "tokens": tokens, "cotangent": cotangent, "gain": gain, "glob": glob, "momentum": momentum, "prev_global": prev_global}


inner_rate = 0.5
outer_rate = 0.7
nesterov = 0.9
mix_weight = 0.5
eps = 1e-06

def one_replica(items):
    weights, inputs, grads_in, gain = items
    x = inputs.astype(jnp.float32)
    inv = lax.rsqrt(lax.optimization_barrier(jnp.mean(x * x, axis=-1, keepdims=True)) + eps)
    unit = x * inv
    normed = (unit * gain).astype(jnp.bfloat16)
    blocks_n = normed.reshape(N_FSDP, TOK_DEV, D).astype(jnp.float32)
    blocks_v = grads_in.reshape(N_FSDP, TOK_DEV, HV).astype(jnp.float32)
    partial_terms = jnp.einsum('std,sth->sdh', blocks_n, blocks_v).astype(jnp.bfloat16)
    grad = lax.optimization_barrier(jnp.sum(partial_terms.astype(jnp.float32), axis=0))
    updated = (weights.astype(jnp.float32) - inner_rate * grad).astype(jnp.bfloat16)
    dn = jnp.dot(grads_in, weights.T, preferred_element_type=jnp.float32)
    scaled = gain * dn
    grad_tokens = (inv * (scaled - unit * lax.optimization_barrier(jnp.mean(unit * scaled, axis=-1, keepdims=True)))).astype(jnp.bfloat16)
    return (updated, grad_tokens)

def reference(params, tokens, cotangent, gain, glob, momentum, prev_global):

    def step(items):
        return one_replica((items[0], items[1], items[2], gain))
    updated, grad_tokens = lax.map(step, (params, tokens, cotangent))
    avg = lax.optimization_barrier(jnp.sum(updated.astype(jnp.float32), axis=0)) / REPLICAS
    delta = glob - avg
    new_momentum = nesterov * momentum + delta
    new_global = glob - outer_rate * (delta + nesterov * new_momentum)
    new_params = ((1.0 - mix_weight) * updated.astype(jnp.float32) + mix_weight * prev_global[None]).astype(jnp.bfloat16)
    return (new_params, grad_tokens, new_global, new_momentum)
```

```python
import jax
import jax.numpy as jnp
from jax import lax
from jax.experimental import pallas as pl
from jax.experimental.pallas import tpu as pltpu
from jax.sharding import PartitionSpec as P

inner_rate = 0.5
outer_rate = 0.7
nesterov = 0.9
mix_weight = 0.5
eps = 1e-06

MESH = pl.DeviceIdType.MESH
F32 = jnp.float32
BF16 = jnp.bfloat16

D = 4608
HV = 1024
T = 512
Q = 1152
S = 576
NC = 4
CW = HV // NC
NT = 8
TR = T // NT
NZ = 4
ZR = S // NZ
YR = S // 4
WR = 40
OWN = 18
PZ = 48


def kernel(
    params, tokens, cot, gain, glob, mom, prev,
    new_params, grad_tokens, new_global, new_momentum,
    tok, cc, invb, gb, nst, nnt, wg, gs, gr, gk, zs, zr, up, cr, s2, yr, s8, lr, tot,
    xs, xr, xo, po, pz, pzr, pa, pfull,
    a_s, a_r, b_s, b_r, z_s, z_r, c_s, c_r, y_s, y_r, l_s, l_r, loc, outs,
):
    rep = lax.axis_index("replica")
    fs = lax.axis_index("fsdp")
    core = lax.rem(rep, 2)
    zl = lax.rem(lax.div(rep, 2), 4)
    y = lax.div(rep, 8)
    x = lax.rem(fs, 4)
    zh = lax.div(fs, 4)
    half = lax.div(x, 2)
    par = lax.rem(x, 2)

    dev_a = (rep, zh * 4 + lax.rem(jnp.where(par == 0, x + 3, x + 1), 4))
    dev_b = (rep, zh * 4 + half * 2 + (1 - par))
    dev_z = (rep, (1 - zh) * 4 + x)
    dev_c = ((y * 4 + zl) * 2 + (1 - core), fs)
    dev_y = [((lax.rem(y + d, 4) * 4 + zl) * 2 + core, fs) for d in (1, 2, 3)]
    dev_l = [((y * 4 + lax.rem(zl + d, 4)) * 2 + core, fs) for d in (1, 2, 3)]

    def remote(src, dst, sends, recvs, i, dev):
        return pltpu.make_async_remote_copy(
            src_ref=src,
            dst_ref=dst,
            send_sem=sends.at[i],
            recv_sem=recvs.at[i],
            device_id=dev,
            device_id_type=MESH,
        )

    def column(b):
        plane = (1 - zh) if b % 2 == 0 else zh
        side = (1 - half) if b < 2 else half
        return pl.multiple_of(plane * (D // 2) + side * Q, 128)

    my_rows = pl.multiple_of(par * S, 64)
    its_rows = pl.multiple_of((1 - par) * S, 64)

    loads = [
        pltpu.make_async_copy(tokens.at[:, pl.ds(column(b), Q)], tok.at[b], loc.at[b])
        for b in range(4)
    ]
    load_cot = pltpu.make_async_copy(cot, cc.at[pl.ds(0, T)], loc.at[4])
    load_w = pltpu.make_async_copy(params, wg.at[1, pl.ds(my_rows, S)], loc.at[5])

    barrier = pltpu.get_barrier_semaphore()
    peers = [dev_a, dev_b, dev_z, dev_c] + dev_y + dev_l
    for dev in peers:
        pl.semaphore_signal(barrier, inc=1, device_id=dev, device_id_type=MESH)
    for cp in loads:
        cp.start()
    load_cot.start()
    load_w.start()
    pl.semaphore_wait(barrier, len(peers))

    send_cot = remote(cot, cc.at[pl.ds(T, T)], a_s, a_r, 0, dev_a)
    send_cot.start()
    send_w = remote(params, wg.at[1, pl.ds(my_rows, S)], b_s, b_r, 0, dev_b)
    send_w.start()
    far_w = [
        remote(
            params.at[pl.ds(k * ZR, ZR)],
            wg.at[0, pl.ds(pl.multiple_of(my_rows + k * ZR, 16), ZR)],
            z_s, z_r, k, dev_z,
        )
        for k in range(NZ)
    ]
    for cp in far_w:
        cp.start()
    send_prev = remote(prev, po, c_s, c_r, 0, dev_c)
    send_prev.start()

    for b in range(4):
        gb[b] = gain[:, pl.ds(column(b), Q)]
    for cp in loads:
        cp.wait()

    @pl.loop(0, T // 32)
    def _(i):
        rows = pl.ds(pl.multiple_of(i * 32, 32), 32)
        acc = jnp.zeros((32, 128), F32)
        for b in range(4):
            for j in range(Q // 128):
                v = tok[b, rows, j * 128 : (j + 1) * 128].astype(F32)
                acc = acc + v * v
        inv = lax.rsqrt(jnp.sum(acc, axis=-1, keepdims=True) * (1.0 / D) + eps)
        invb[rows, :] = jnp.broadcast_to(inv, (32, 128))

    def normed(b, put):
        @pl.loop(0, Q // 128)
        def _(j):
            cols = pl.ds(pl.multiple_of(j * 128, 128), 128)
            v = tok[b, :, cols].astype(F32) * invb[...] * gb[b, :, cols]
            put(cols, v.T.astype(BF16))

    def put_send(o):
        def put(rows, v):
            nst[o, rows, :] = v
        return put

    def put_own(o):
        def put(rows, v):
            nnt[o, rows, 0:T] = v
        return put

    send_n = []
    for o in range(2):
        normed(o, put_send(o))
        for p, start in enumerate((my_rows, its_rows)):
            rows = pl.ds(start, S)
            cp = remote(nst.at[o, rows], nnt.at[o, rows, pl.ds(T, T)], a_s, a_r, 1 + 2 * o + p, dev_a)
            cp.start()
            send_n.append(cp)

    send_prev.wait_recv()
    wide = pl.ds(pl.multiple_of(core * (HV // 2), 128), HV // 2)
    pz[...] = jnp.zeros_like(pz)

    @pl.when(core == 0)
    def _():
        pz[0:OWN, :] = prev[:, wide]
        pz[OWN : 2 * OWN, :] = po[:, wide]

    @pl.when(core == 1)
    def _():
        pz[0:OWN, :] = po[:, wide]
        pz[OWN : 2 * OWN, :] = prev[:, wide]

    pzr[zl] = pz[...].astype(BF16)
    prev_l = [remote(pzr.at[zl], pzr.at[zl], l_s, l_r, d, dev_l[d]) for d in range(3)]
    for cp in prev_l:
        cp.start()

    for o in range(2):
        normed(2 + o, put_own(o))

    for cp in prev_l:
        cp.wait_recv()
    for k in range(4):
        pa[k * 36 : (k + 1) * 36, :] = pzr[k, 0:36, :].astype(F32)
    y_rows = pl.ds(pl.multiple_of(y * YR, 16), YR)
    pfull[core, y_rows, :] = pa[...].astype(BF16)
    prev_y = [
        remote(pfull.at[core, y_rows], pfull.at[core, y_rows], y_s, y_r, d, dev_y[d])
        for d in range(3)
    ]
    for cp in prev_y:
        cp.start()

    forward = [
        remote(
            wg.at[0, pl.ds(pl.multiple_of(my_rows + k * ZR, 16), ZR)],
            wg.at[0, pl.ds(pl.multiple_of(my_rows + k * ZR, 16), ZR)],
            b_s, b_r, 1 + k, dev_b,
        )
        for k in range(NZ)
    ]

    def pass_on(k):
        far_w[k].wait_recv()
        forward[k].start()

    def send_g(o, c):
        return remote(gs.at[o, c], gr.at[o, c], b_s, b_r, 5 + NC * o + c, dev_b)

    def product(o, rows, c):
        cols = pl.ds(pl.multiple_of(c * CW, 128), CW)
        return jnp.dot(nnt[o, pl.ds(rows, S), :], cc[:, cols], preferred_element_type=F32)

    def give(o):
        send_n[2 * o].wait_recv()

        @pl.loop(0, NC)
        def _(c):
            gs[o, c] = product(o, its_rows, c).astype(BF16)
            send_g(o, c).start()

    def keep(o):
        send_n[2 * o + 1].wait_recv()

        @pl.loop(0, NC)
        def _(c):
            gk[o, c] = product(o, my_rows, c)

    def send_s(c):
        return remote(zs.at[c], zr.at[c], z_s, z_r, NZ + c, dev_z)

    def far_sum(c):
        send_g(0, c).wait_recv()
        zs[c] = (gk[0, c] + gr[0, c].astype(F32)).astype(BF16)
        send_s(c).start()

    pass_on(0)
    for cp in prev_y:
        cp.wait_recv()
    prev_c = remote(pfull.at[core], pfull.at[core], c_s, c_r, 1, dev_c)
    prev_c.start()
    pass_on(1)
    load_cot.wait()
    load_w.wait()
    send_cot.wait_recv()
    give(0)
    pass_on(2)
    keep(0)
    pass_on(3)
    far_sum(0)
    far_sum(1)
    give(1)
    far_sum(2)
    far_sum(3)

    send_w.wait_recv()
    for cp in forward:
        cp.wait_recv()

    def dn(first, put):
        for o in range(2):

            @pl.loop(0, 3)
            def _(n):
                rows = pl.ds(pl.multiple_of(n * 384, 128), 384)
                cols = pl.ds(pl.multiple_of(o * Q + n * 384, 128), 384)
                put(
                    cols,
                    lax.dot_general(
                        cc[first : first + T, :],
                        wg[o, rows, :],
                        (((1,), (1,)), ((), ())),
                        preferred_element_type=F32,
                    ),
                )

    def put_xs(cols, v):
        xs[:, cols] = v.astype(BF16)

    def put_xo(cols, v):
        xo[:, cols] = v

    dn(T, put_xs)
    send_x = []
    for t in range(NT):
        rows = pl.ds(t * TR, TR)
        cp = remote(xs.at[rows], xr.at[rows], a_s, a_r, 5 + t, dev_a)
        cp.start()
        send_x.append(cp)
    keep(1)
    dn(0, put_xo)

    stores = []

    def finish(t):
        send_x[t].wait_recv()

        @pl.loop(0, TR // 16)
        def _(i):
            rows = pl.ds(pl.multiple_of(t * TR + i * 16, 16), 16)
            inv = invb[rows, :]

            def parts(b, j):
                cols = slice(j * 128, (j + 1) * 128)
                unit = tok[b, rows, cols].astype(F32) * inv
                at = (b % 2) * Q + j * 128
                if b < 2:
                    d = xr[rows, at : at + 128].astype(F32)
                else:
                    d = xo[rows, at : at + 128]
                return unit, gb[b, :, cols] * d

            acc = jnp.zeros((16, 128), F32)
            for b in range(4):
                for j in range(Q // 128):
                    unit, scaled = parts(b, j)
                    acc = acc + unit * scaled
            mean = jnp.sum(acc, axis=-1, keepdims=True) * (1.0 / D)
            for b in range(4):
                for j in range(Q // 128):
                    unit, scaled = parts(b, j)
                    tok[b, rows, j * 128 : (j + 1) * 128] = (inv * (scaled - unit * mean)).astype(BF16)

        for b in range(4):
            cp = pltpu.make_async_copy(
                tok.at[b, pl.ds(t * TR, TR)],
                grad_tokens.at[pl.ds(t * TR, TR), pl.ds(column(b), Q)],
                outs.at[t, b],
            )
            cp.start()
            stores.append(cp)

    def send_up(c):
        return remote(up.at[2 * c + 1 - core], cr.at[c], c_s, c_r, 2 + c, dev_c)

    def send_y(c, d):
        rows = pl.ds(pl.multiple_of(lax.rem(y + d + 1, 4) * YR, 16), YR)
        return remote(s2.at[c, rows], yr.at[c, d], y_s, y_r, 3 + 3 * c + d, dev_y[d])

    def window(pos):
        return pl.multiple_of(pos * 36 - lax.rem(pos, 2) * 4, 8)

    def send_l(c, d):
        rows = pl.ds(window(lax.rem(zl + d + 1, 4)), WR)
        return remote(s8.at[c, rows], lr.at[c, d], l_s, l_r, 3 + 3 * c + d, dev_l[d])

    def send_tot(c):
        return remote(tot.at[2 * c + core], tot.at[2 * c + core], c_s, c_r, 6 + c, dev_c)

    def update(c):
        if c == 0:
            prev_c.wait_recv()
        send_g(1, c).wait_recv()
        send_s(c).wait_recv()
        for k in range(2):
            part = slice(k * 128, (k + 1) * 128)
            cols = slice(c * CW + k * 128, c * CW + (k + 1) * 128)
            grad = gk[1, c, :, part] + gr[1, c, :, part].astype(F32) + zr[c, :, part].astype(F32)
            now = (wg[1, pl.ds(my_rows, S), cols].astype(F32) - inner_rate * grad).astype(BF16)
            up[2 * c + k] = now
        send_up(c).start()
        for k in range(2):
            cols = slice(c * CW + k * 128, c * CW + (k + 1) * 128)
            at = (c % 2) * CW + k * 128
            old = pfull[c // 2, :, at : at + 128].astype(F32)
            new_params[:, cols] = (
                (1.0 - mix_weight) * up[2 * c + k].astype(F32) + mix_weight * old
            ).astype(BF16)

    def both_cores(c):
        send_up(c).wait_recv()
        s2[c] = up[2 * c + core].astype(F32) + cr[c].astype(F32)
        for d in range(3):
            send_y(c, d).start()

    def all_y(c):
        for d in range(3):
            send_y(c, d).wait_recv()
        s8[c] = s2[c, y_rows, :] + yr[c, 0] + yr[c, 1] + yr[c, 2]
        for d in range(3):
            send_l(c, d).start()

    def all_l(c):
        for d in range(3):
            send_l(c, d).wait_recv()
        tot[2 * c + core] = s8[c, pl.ds(window(zl), WR), :] + lr[c, 0] + lr[c, 1] + lr[c, 2]
        send_tot(c).start()

    update(0)
    finish(0)
    both_cores(0)
    finish(1)
    all_y(0)
    update(1)
    finish(2)
    all_l(0)
    both_cores(1)
    finish(3)
    all_y(1)
    update(2)
    finish(4)
    all_l(1)
    both_cores(2)
    update(3)
    finish(5)
    all_y(2)
    both_cores(3)
    finish(6)
    all_l(2)
    all_y(3)
    all_l(3)

    for c in range(NC):
        send_tot(c).wait_recv()
    place = lax.rem(zl, 2) * 2 + core
    for j in range(HV // 128):
        cols = slice(j * 128, (j + 1) * 128)
        total = jnp.where(
            place < 2,
            jnp.where(place == 0, tot[j, 0:18, :], tot[j, 18:36, :]),
            jnp.where(place == 2, tot[j, 4:22, :], tot[j, 22:40, :]),
        )
        delta = glob[:, cols] - total * (1.0 / 32)
        moved = nesterov * mom[:, cols] + delta
        new_momentum[:, cols] = moved
        new_global[:, cols] = glob[:, cols] - outer_rate * (delta + nesterov * moved)
    finish(7)

    for cp in [send_cot, send_w, send_prev, prev_c] + far_w + forward + send_n + send_x + prev_l + prev_y:
        cp.wait_send()
    for c in range(NC):
        send_g(0, c).wait_send()
        send_g(1, c).wait_send()
        send_s(c).wait_send()
        send_up(c).wait_send()
        send_tot(c).wait_send()
        for d in range(3):
            send_y(c, d).wait_send()
            send_l(c, d).wait_send()
    for cp in stores:
        cp.wait()


def shards(params, tokens, cotangent, gain, glob, momentum, prev_global):
    vmem = pl.BlockSpec(memory_space=pltpu.VMEM)
    hbm = pl.BlockSpec(memory_space=pl.ANY)
    dma = pltpu.SemaphoreType.DMA
    out = pl.pallas_call(
        kernel,
        out_shape=(
            jax.ShapeDtypeStruct((S, HV), BF16),
            jax.ShapeDtypeStruct((T, D), BF16),
            jax.ShapeDtypeStruct((OWN, HV), F32),
            jax.ShapeDtypeStruct((OWN, HV), F32),
        ),
        in_specs=[hbm, hbm, hbm, vmem, vmem, vmem, vmem],
        out_specs=(vmem, hbm, vmem, vmem),
        scratch_shapes=[
            pltpu.VMEM((4, T, Q), BF16),
            pltpu.VMEM((2 * T, HV), BF16),
            pltpu.VMEM((T, 128), F32),
            pltpu.VMEM((4, 1, Q), F32),
            pltpu.VMEM((2, Q, T), BF16),
            pltpu.VMEM((2, Q, 2 * T), BF16),
            pltpu.VMEM((2, Q, HV), BF16),
            pltpu.VMEM((2, NC, S, CW), BF16),
            pltpu.VMEM((2, NC, S, CW), BF16),
            pltpu.VMEM((2, NC, S, CW), F32),
            pltpu.VMEM((NC, S, CW), BF16),
            pltpu.VMEM((NC, S, CW), BF16),
            pltpu.VMEM((2 * NC, S, 128), BF16),
            pltpu.VMEM((NC, S, 128), BF16),
            pltpu.VMEM((NC, S, 128), F32),
            pltpu.VMEM((NC, 3, YR, 128), F32),
            pltpu.VMEM((NC, YR, 128), F32),
            pltpu.VMEM((NC, 3, WR, 128), F32),
            pltpu.VMEM((2 * NC, WR, 128), F32),
            pltpu.VMEM((T, 2 * Q), BF16),
            pltpu.VMEM((T, 2 * Q), BF16),
            pltpu.VMEM((T, 2 * Q), F32),
            pltpu.VMEM((OWN, HV), F32),
            pltpu.VMEM((PZ, HV // 2), F32),
            pltpu.VMEM((4, PZ, HV // 2), BF16),
            pltpu.VMEM((YR, HV // 2), F32),
            pltpu.VMEM((2, S, HV // 2), BF16),
            dma((5 + NT,)), dma((5 + NT,)),
            dma((5 + 2 * NC,)), dma((5 + 2 * NC,)),
            dma((NZ + NC,)), dma((NZ + NC,)),
            dma((2 + 2 * NC,)), dma((2 + 2 * NC,)),
            dma((3 + 3 * NC,)), dma((3 + 3 * NC,)),
            dma((3 + 3 * NC,)), dma((3 + 3 * NC,)),
            dma((6,)),
            dma((NT, 4)),
        ],
        compiler_params=pltpu.CompilerParams(
            collective_id=0, has_side_effects=True, vmem_limit_bytes=60 * 1024 * 1024
        ),
        cost_estimate=pl.CostEstimate(
            flops=4 * T * D * HV, bytes_accessed=16 * 1024 * 1024, transcendentals=T
        ),
        name="diloco",
    )(params[0], tokens[0], cotangent[0], gain.reshape(1, D), glob, momentum, prev_global)
    return (out[0][None], out[1][None], out[2], out[3])


def solution(mesh):
    placed = (
        P("replica", "fsdp", None),
        P("replica", "fsdp", None),
        P("replica", "fsdp", None),
        P(),
        P(("fsdp", "replica"), None),
        P(("fsdp", "replica"), None),
        P(("fsdp", "replica"), None),
    )
    return jax.shard_map(
        shards,
        mesh=mesh,
        in_specs=placed,
        out_specs=(
            P("replica", "fsdp", None),
            P("replica", "fsdp", None),
            P(("fsdp", "replica"), None),
            P(("fsdp", "replica"), None),
        ),
        check_vma=False,
    )
```

```python
import jax
import jax.numpy as jnp
from jax import lax
from jax.experimental import pallas as pl
from jax.experimental.pallas import tpu as pltpu
from jax.sharding import PartitionSpec as P

inner_rate = 0.5
outer_rate = 0.7
nesterov = 0.9
mix_weight = 0.5
eps = 1e-06

MESH = pl.DeviceIdType.MESH
F32 = jnp.float32
BF16 = jnp.bfloat16

D = 4608
HV = 1024
T = 512
Q = 1152
S = 576
NC = 4
CW = HV // NC
NT = 8
TR = T // NT
NZ = 4
ZR = S // NZ
YR = S // 4
WR = 40
OWN = 18
PZ = 48


def kernel(
    params, tokens, cot, gain, glob, mom, prev,
    new_params, tok, new_global, new_momentum,
    cc, invb, gb, nst, nnt, wg, gs, gr, gk, zs, zr, up, cr, s2, yr, s8, lr, tot,
    xs, xr, xo, po, pz, pzr, pa, pfull,
    a_s, a_r, b_s, b_r, z_s, z_r, c_s, c_r, y_s, y_r, l_s, l_r, loc,
):
    rep = lax.axis_index("replica")
    fs = lax.axis_index("fsdp")
    core = lax.rem(rep, 2)
    zl = lax.rem(lax.div(rep, 2), 4)
    y = lax.div(rep, 8)
    x = lax.rem(fs, 4)
    zh = lax.div(fs, 4)
    half = lax.div(x, 2)
    par = lax.rem(x, 2)

    dev_a = (rep, zh * 4 + lax.rem(jnp.where(par == 0, x + 3, x + 1), 4))
    dev_b = (rep, zh * 4 + half * 2 + (1 - par))
    dev_z = (rep, (1 - zh) * 4 + x)
    dev_c = ((y * 4 + zl) * 2 + (1 - core), fs)
    dev_y = [((lax.rem(y + d, 4) * 4 + zl) * 2 + core, fs) for d in (1, 2, 3)]
    dev_l = [((y * 4 + lax.rem(zl + d, 4)) * 2 + core, fs) for d in (1, 2, 3)]

    def remote(src, dst, sends, recvs, i, dev):
        return pltpu.make_async_remote_copy(
            src_ref=src,
            dst_ref=dst,
            send_sem=sends.at[i],
            recv_sem=recvs.at[i],
            device_id=dev,
            device_id_type=MESH,
        )

    def column(b):
        plane = (1 - zh) if b % 2 == 0 else zh
        side = (1 - half) if b < 2 else half
        return pl.multiple_of(plane * (D // 2) + side * Q, 128)

    def tile(b, j):
        return pl.ds(pl.multiple_of(column(b) + j * 128, 128), 128)

    my_rows = pl.multiple_of(par * S, 64)
    its_rows = pl.multiple_of((1 - par) * S, 64)

    loads = [
        pltpu.make_async_copy(
            tokens.at[:, pl.ds(column(b), Q)], tok.at[:, pl.ds(column(b), Q)], loc.at[b]
        )
        for b in range(4)
    ]
    load_cot = pltpu.make_async_copy(cot, cc.at[pl.ds(0, T)], loc.at[4])
    load_w = pltpu.make_async_copy(params, wg.at[1, pl.ds(my_rows, S)], loc.at[5])

    barrier = pltpu.get_barrier_semaphore()
    peers = [dev_a, dev_b, dev_z, dev_c] + dev_y + dev_l
    for dev in peers:
        pl.semaphore_signal(barrier, inc=1, device_id=dev, device_id_type=MESH)
    for cp in loads:
        cp.start()
    load_cot.start()
    load_w.start()
    pl.semaphore_wait(barrier, len(peers))

    send_prev = remote(prev, po, c_s, c_r, 0, dev_c)
    send_prev.start()
    send_cot = remote(cot, cc.at[pl.ds(T, T)], a_s, a_r, 0, dev_a)
    send_cot.start()
    send_w = remote(params, wg.at[1, pl.ds(my_rows, S)], b_s, b_r, 0, dev_b)
    send_w.start()
    far_w = [
        remote(
            params.at[pl.ds(k * ZR, ZR)],
            wg.at[0, pl.ds(pl.multiple_of(my_rows + k * ZR, 16), ZR)],
            z_s, z_r, k, dev_z,
        )
        for k in range(NZ)
    ]
    for cp in far_w:
        cp.start()

    send_prev.wait_recv()
    wide = pl.ds(pl.multiple_of(core * (HV // 2), 128), HV // 2)
    pz[...] = jnp.zeros_like(pz)

    @pl.when(core == 0)
    def _():
        pz[0:OWN, :] = prev[:, wide]
        pz[OWN : 2 * OWN, :] = po[:, wide]

    @pl.when(core == 1)
    def _():
        pz[0:OWN, :] = po[:, wide]
        pz[OWN : 2 * OWN, :] = prev[:, wide]

    pzr[zl] = pz[...].astype(BF16)
    prev_l = [remote(pzr.at[zl], pzr.at[zl], l_s, l_r, d, dev_l[d]) for d in range(3)]
    for cp in prev_l:
        cp.start()

    for b in range(4):
        gb[b] = gain[:, pl.ds(column(b), Q)]
    for cp in loads:
        cp.wait()

    @pl.loop(0, T // 32)
    def _(i):
        rows = pl.ds(pl.multiple_of(i * 32, 32), 32)
        acc = jnp.zeros((32, 128), F32)
        for b in range(4):
            for j in range(Q // 128):
                v = tok[rows, tile(b, j)].astype(F32)
                acc = acc + v * v
        inv = lax.rsqrt(jnp.sum(acc, axis=-1, keepdims=True) * (1.0 / D) + eps)
        invb[rows, :] = jnp.broadcast_to(inv, (32, 128))

    def normed(b, put):
        @pl.loop(0, Q // 128)
        def _(j):
            cols = pl.ds(pl.multiple_of(j * 128, 128), 128)
            v = tok[:, tile(b, j)].astype(F32) * invb[...] * gb[b, :, cols]
            put(cols, v.T.astype(BF16))

    def put_send(o):
        def put(rows, v):
            nst[o, rows, :] = v
        return put

    def put_own(o):
        def put(rows, v):
            nnt[o, rows, 0:T] = v
        return put

    send_n = []
    for o in range(2):
        normed(o, put_send(o))
        for p, start in enumerate((my_rows, its_rows)):
            rows = pl.ds(start, S)
            cp = remote(nst.at[o, rows], nnt.at[o, rows, pl.ds(T, T)], a_s, a_r, 1 + 2 * o + p, dev_a)
            cp.start()
            send_n.append(cp)

    for o in range(2):
        normed(2 + o, put_own(o))

    y_rows = pl.ds(pl.multiple_of(y * YR, 16), YR)
    prev_y = []

    def prev_to_y():
        for cp in prev_l:
            cp.wait_recv()
        for k in range(4):
            pa[k * 36 : (k + 1) * 36, :] = pzr[k, 0:36, :].astype(F32)
        pfull[core, y_rows, :] = pa[...].astype(BF16)
        prev_y.extend(
            [
                remote(pfull.at[core, y_rows], pfull.at[core, y_rows], y_s, y_r, d, dev_y[d])
                for d in range(3)
            ]
        )
        for cp in prev_y:
            cp.start()

    forward = [
        remote(
            wg.at[0, pl.ds(pl.multiple_of(my_rows + k * ZR, 16), ZR)],
            wg.at[0, pl.ds(pl.multiple_of(my_rows + k * ZR, 16), ZR)],
            b_s, b_r, 1 + k, dev_b,
        )
        for k in range(NZ)
    ]

    def pass_on(k):
        far_w[k].wait_recv()
        forward[k].start()

    def send_g(o, c):
        return remote(gs.at[o, c], gr.at[o, c], b_s, b_r, 5 + NC * o + c, dev_b)

    def product(o, rows, c):
        cols = pl.ds(pl.multiple_of(c * CW, 128), CW)
        return jnp.dot(nnt[o, pl.ds(rows, S), :], cc[:, cols], preferred_element_type=F32)

    def give(o):
        send_n[2 * o].wait_recv()

        @pl.loop(0, NC)
        def _(c):
            gs[o, c] = product(o, its_rows, c).astype(BF16)
            send_g(o, c).start()

    def keep(o):
        send_n[2 * o + 1].wait_recv()

        @pl.loop(0, NC)
        def _(c):
            gk[o, c] = product(o, my_rows, c)

    def send_s(c):
        return remote(zs.at[c], zr.at[c], z_s, z_r, NZ + c, dev_z)

    def far_sum(c):
        send_g(0, c).wait_recv()
        zs[c] = (gk[0, c] + gr[0, c].astype(F32)).astype(BF16)
        send_s(c).start()

    def dn(o, first, put):
        @pl.loop(0, 3)
        def _(n):
            rows = pl.ds(pl.multiple_of(n * 384, 128), 384)
            cols = pl.ds(pl.multiple_of(o * Q + n * 384, 128), 384)
            put(
                cols,
                lax.dot_general(
                    cc[first : first + T, :],
                    wg[o, rows, :],
                    (((1,), (1,)), ((), ())),
                    preferred_element_type=F32,
                ),
            )

    def put_xs(cols, v):
        xs[:, cols] = v.astype(BF16)

    def put_xo(cols, v):
        xo[:, cols] = v

    own_plane = pl.ds(Q, Q)
    send_x1 = remote(xs.at[:, own_plane], xr.at[:, own_plane], a_s, a_r, 5 + NT, dev_a)
    send_x = []
    for t in range(NT):
        at = (pl.ds(t * TR, TR), pl.ds(0, Q))
        send_x.append(remote(xs.at[at], xr.at[at], a_s, a_r, 5 + t, dev_a))

    def finish(t):
        send_x[t].wait_recv()

        @pl.loop(0, TR // 16)
        def _(i):
            rows = pl.ds(pl.multiple_of(t * TR + i * 16, 16), 16)
            inv = invb[rows, :]

            def parts(b, j):
                cols = slice(j * 128, (j + 1) * 128)
                unit = tok[rows, tile(b, j)].astype(F32) * inv
                at = (b % 2) * Q + j * 128
                if b < 2:
                    d = xr[rows, at : at + 128].astype(F32)
                else:
                    d = xo[rows, at : at + 128]
                return unit, gb[b, :, cols] * d

            acc = jnp.zeros((16, 128), F32)
            for b in range(4):
                for j in range(Q // 128):
                    unit, scaled = parts(b, j)
                    acc = acc + unit * scaled
            mean = jnp.sum(acc, axis=-1, keepdims=True) * (1.0 / D)
            for b in range(4):
                for j in range(Q // 128):
                    unit, scaled = parts(b, j)
                    tok[rows, tile(b, j)] = (inv * (scaled - unit * mean)).astype(BF16)

    def send_up(c):
        return remote(up.at[2 * c + 1 - core], cr.at[c], c_s, c_r, 2 + c, dev_c)

    def send_y(c, d):
        rows = pl.ds(pl.multiple_of(lax.rem(y + d + 1, 4) * YR, 16), YR)
        return remote(s2.at[c, rows], yr.at[c, d], y_s, y_r, 3 + 3 * c + d, dev_y[d])

    def window(pos):
        return pl.multiple_of(pos * 36 - lax.rem(pos, 2) * 4, 8)

    def send_l(c, d):
        rows = pl.ds(window(lax.rem(zl + d + 1, 4)), WR)
        return remote(s8.at[c, rows], lr.at[c, d], l_s, l_r, 3 + 3 * c + d, dev_l[d])

    def send_tot(c):
        return remote(tot.at[2 * c + core], tot.at[2 * c + core], c_s, c_r, 6 + c, dev_c)

    def update(c):
        send_g(1, c).wait_recv()
        send_s(c).wait_recv()
        for k in range(2):
            part = slice(k * 128, (k + 1) * 128)
            cols = slice(c * CW + k * 128, c * CW + (k + 1) * 128)
            grad = gk[1, c, :, part] + gr[1, c, :, part].astype(F32) + zr[c, :, part].astype(F32)
            now = (wg[1, pl.ds(my_rows, S), cols].astype(F32) - inner_rate * grad).astype(BF16)
            up[2 * c + k] = now
        send_up(c).start()

    def mix(c):
        for k in range(2):
            cols = slice(c * CW + k * 128, c * CW + (k + 1) * 128)
            at = (c % 2) * CW + k * 128
            old = pfull[c // 2, :, at : at + 128].astype(F32)
            new_params[:, cols] = (
                (1.0 - mix_weight) * up[2 * c + k].astype(F32) + mix_weight * old
            ).astype(BF16)

    def both_cores(c):
        send_up(c).wait_recv()
        s2[c] = up[2 * c + core].astype(F32) + cr[c].astype(F32)
        for d in range(3):
            send_y(c, d).start()

    def all_y(c):
        for d in range(3):
            send_y(c, d).wait_recv()
        s8[c] = s2[c, y_rows, :] + yr[c, 0] + yr[c, 1] + yr[c, 2]
        for d in range(3):
            send_l(c, d).start()

    def all_l(c):
        for d in range(3):
            send_l(c, d).wait_recv()
        tot[2 * c + core] = s8[c, pl.ds(window(zl), WR), :] + lr[c, 0] + lr[c, 1] + lr[c, 2]
        send_tot(c).start()

    pass_on(0)
    pass_on(1)
    load_cot.wait()
    load_w.wait()
    send_cot.wait_recv()
    give(0)
    send_w.wait_recv()
    dn(1, T, put_xs)
    send_x1.start()
    pass_on(2)
    keep(0)
    far_sum(0)
    far_sum(1)
    pass_on(3)
    far_sum(2)
    give(1)
    far_sum(3)
    dn(1, 0, put_xo)
    keep(1)
    for cp in forward:
        cp.wait_recv()
    dn(0, T, put_xs)
    for cp in send_x:
        cp.start()
    dn(0, 0, put_xo)

    update(0)
    both_cores(0)
    update(1)
    all_y(0)
    both_cores(1)
    update(2)
    all_y(1)
    both_cores(2)
    send_x1.wait_recv()
    finish(0)
    all_y(2)
    finish(1)
    finish(2)
    finish(3)
    update(3)
    finish(4)
    both_cores(3)
    prev_to_y()
    finish(5)
    all_y(3)
    all_l(0)
    all_l(1)
    all_l(2)
    for cp in prev_y:
        cp.wait_recv()
    prev_c = remote(pfull.at[core], pfull.at[core], c_s, c_r, 1, dev_c)
    prev_c.start()
    finish(6)
    all_l(3)
    prev_c.wait_recv()
    for c in range(NC):
        mix(c)

    for c in range(NC):
        send_tot(c).wait_recv()
    place = lax.rem(zl, 2) * 2 + core
    for j in range(HV // 128):
        cols = slice(j * 128, (j + 1) * 128)
        total = jnp.where(
            place < 2,
            jnp.where(place == 0, tot[j, 0:18, :], tot[j, 18:36, :]),
            jnp.where(place == 2, tot[j, 4:22, :], tot[j, 22:40, :]),
        )
        delta = glob[:, cols] - total * (1.0 / 32)
        moved = nesterov * mom[:, cols] + delta
        new_momentum[:, cols] = moved
        new_global[:, cols] = glob[:, cols] - outer_rate * (delta + nesterov * moved)
    finish(7)

    for cp in [send_cot, send_w, send_prev, prev_c, send_x1] + far_w + forward + send_n + send_x + prev_l + prev_y:
        cp.wait_send()
    for c in range(NC):
        send_g(0, c).wait_send()
        send_g(1, c).wait_send()
        send_s(c).wait_send()
        send_up(c).wait_send()
        send_tot(c).wait_send()
        for d in range(3):
            send_y(c, d).wait_send()
            send_l(c, d).wait_send()


def shards(params, tokens, cotangent, gain, glob, momentum, prev_global):
    vmem = pl.BlockSpec(memory_space=pltpu.VMEM)
    hbm = pl.BlockSpec(memory_space=pl.ANY)
    dma = pltpu.SemaphoreType.DMA
    out = pl.pallas_call(
        kernel,
        out_shape=(
            pltpu.VMEM((S, HV), BF16),
            pltpu.VMEM((T, D), BF16),
            pltpu.VMEM((OWN, HV), F32),
            pltpu.VMEM((OWN, HV), F32),
        ),
        in_specs=[hbm, hbm, hbm, vmem, vmem, vmem, vmem],
        out_specs=(vmem, vmem, vmem, vmem),
        scratch_shapes=[
            pltpu.VMEM((2 * T, HV), BF16),
            pltpu.VMEM((T, 128), F32),
            pltpu.VMEM((4, 1, Q), F32),
            pltpu.VMEM((2, Q, T), BF16),
            pltpu.VMEM((2, Q, 2 * T), BF16),
            pltpu.VMEM((2, Q, HV), BF16),
            pltpu.VMEM((2, NC, S, CW), BF16),
            pltpu.VMEM((2, NC, S, CW), BF16),
            pltpu.VMEM((2, NC, S, CW), F32),
            pltpu.VMEM((NC, S, CW), BF16),
            pltpu.VMEM((NC, S, CW), BF16),
            pltpu.VMEM((2 * NC, S, 128), BF16),
            pltpu.VMEM((NC, S, 128), BF16),
            pltpu.VMEM((NC, S, 128), F32),
            pltpu.VMEM((NC, 3, YR, 128), F32),
            pltpu.VMEM((NC, YR, 128), F32),
            pltpu.VMEM((NC, 3, WR, 128), F32),
            pltpu.VMEM((2 * NC, WR, 128), F32),
            pltpu.VMEM((T, 2 * Q), BF16),
            pltpu.VMEM((T, 2 * Q), BF16),
            pltpu.VMEM((T, 2 * Q), F32),
            pltpu.VMEM((OWN, HV), F32),
            pltpu.VMEM((PZ, HV // 2), F32),
            pltpu.VMEM((4, PZ, HV // 2), BF16),
            pltpu.VMEM((YR, HV // 2), F32),
            pltpu.VMEM((2, S, HV // 2), BF16),
            dma((6 + NT,)), dma((6 + NT,)),
            dma((5 + 2 * NC,)), dma((5 + 2 * NC,)),
            dma((NZ + NC,)), dma((NZ + NC,)),
            dma((2 + 2 * NC,)), dma((2 + 2 * NC,)),
            dma((3 + 3 * NC,)), dma((3 + 3 * NC,)),
            dma((3 + 3 * NC,)), dma((3 + 3 * NC,)),
            dma((6,)),
        ],
        compiler_params=pltpu.CompilerParams(
            collective_id=0, has_side_effects=True, vmem_limit_bytes=54 * 1024 * 1024
        ),
        cost_estimate=pl.CostEstimate(
            flops=4 * T * D * HV, bytes_accessed=16 * 1024 * 1024, transcendentals=T
        ),
        name="diloco",
    )(params[0], tokens[0], cotangent[0], gain.reshape(1, D), glob, momentum, prev_global)
    return (out[0][None], out[1][None], out[2], out[3])


def solution(mesh):
    placed = (
        P("replica", "fsdp", None),
        P("replica", "fsdp", None),
        P("replica", "fsdp", None),
        P(),
        P(("fsdp", "replica"), None),
        P(("fsdp", "replica"), None),
        P(("fsdp", "replica"), None),
    )
    return jax.shard_map(
        shards,
        mesh=mesh,
        in_specs=placed,
        out_specs=(
            P("replica", "fsdp", None),
            P("replica", "fsdp", None),
            P(("fsdp", "replica"), None),
            P(("fsdp", "replica"), None),
        ),
        check_vma=False,
    )
```

```python
import functools

import jax
import jax.numpy as jnp
from jax import lax
from jax.experimental import pallas as pl
from jax.experimental.pallas import tpu as pltpu
from jax.sharding import PartitionSpec as P

inner_rate = 0.5
outer_rate = 0.7
nesterov = 0.9
mix_weight = 0.5
eps = 1e-06

MESH = pl.DeviceIdType.MESH
F32 = jnp.float32
BF16 = jnp.bfloat16

D = 4608
HV = 1024
T = 512
Q = 1152
S = 576
NC = 4
CW = HV // NC
NT = 8
TR = T // NT
NZ = 4
ZR = S // NZ
YR = S // 4
WR = 40
OWN = 18
PZ = 48


def kernel(
    params, tokens, cot, gain, glob, mom, prev,
    new_params, tok, new_global, new_momentum,
    cc, invb, gv, nst, nnt, wg, gs, gr, gk, zs, zr, up, cr, s2, yr, s8, lr, tot,
    xs, xa, po, pz, pzr, pa, pfull,
    a_s, a_r, b_s, b_r, z_s, z_r, c_s, c_r, y_s, y_r, l_s, l_r, loc,
):
    rep = lax.axis_index("replica")
    fs = lax.axis_index("fsdp")
    core = lax.rem(rep, 2)
    zl = lax.rem(lax.div(rep, 2), 4)
    y = lax.div(rep, 8)
    x = lax.rem(fs, 4)
    zh = lax.div(fs, 4)
    half = lax.div(x, 2)
    par = lax.rem(x, 2)

    dev_a = (rep, zh * 4 + lax.rem(jnp.where(par == 0, x + 3, x + 1), 4))
    dev_b = (rep, zh * 4 + half * 2 + (1 - par))
    dev_z = (rep, (1 - zh) * 4 + x)
    dev_c = ((y * 4 + zl) * 2 + (1 - core), fs)
    dev_y = [((lax.rem(y + d, 4) * 4 + zl) * 2 + core, fs) for d in (1, 2, 3)]
    dev_l = [((y * 4 + lax.rem(zl + d, 4)) * 2 + core, fs) for d in (1, 2, 3)]

    def remote(src, dst, sends, recvs, i, dev):
        return pltpu.make_async_remote_copy(
            src_ref=src,
            dst_ref=dst,
            send_sem=sends.at[i],
            recv_sem=recvs.at[i],
            device_id=dev,
            device_id_type=MESH,
        )

    def column(b):
        plane = (1 - zh) if b % 2 == 0 else zh
        side = (1 - half) if b < 2 else half
        return pl.multiple_of(plane * (D // 2) + side * Q, 128)

    def tile(b, j):
        return pl.ds(pl.multiple_of(column(b) + j * 128, 128), 128)

    my_rows = pl.multiple_of(par * S, 64)
    its_rows = pl.multiple_of((1 - par) * S, 64)

    loads = [
        pltpu.make_async_copy(tokens, tok, loc.at[0]),
        pltpu.make_async_copy(gain, gv.at[0], loc.at[1]),
    ]
    load_cot = pltpu.make_async_copy(cot, cc.at[pl.ds(0, T)], loc.at[2])
    load_w = pltpu.make_async_copy(params, wg.at[1, pl.ds(my_rows, S)], loc.at[3])

    barrier = pltpu.get_barrier_semaphore()
    peers = [dev_a, dev_b, dev_z, dev_c] + dev_y + dev_l
    for dev in peers:
        pl.semaphore_signal(barrier, inc=1, device_id=dev, device_id_type=MESH)
    for cp in loads:
        cp.start()
    load_cot.start()
    load_w.start()
    pl.semaphore_wait(barrier, len(peers))

    send_prev = remote(prev, po, c_s, c_r, 0, dev_c)
    send_prev.start()
    send_cot = remote(cot, cc.at[pl.ds(T, T)], a_s, a_r, 0, dev_a)
    send_cot.start()
    send_w = remote(params, wg.at[1, pl.ds(my_rows, S)], b_s, b_r, 0, dev_b)
    send_w.start()
    far_w = [
        remote(
            params.at[pl.ds(k * ZR, ZR)],
            wg.at[0, pl.ds(pl.multiple_of(my_rows + k * ZR, 16), ZR)],
            z_s, z_r, k, dev_z,
        )
        for k in range(NZ)
    ]
    for cp in far_w:
        cp.start()

    send_prev.wait_recv()
    wide = pl.ds(pl.multiple_of(core * (HV // 2), 128), HV // 2)
    pz[...] = jnp.zeros_like(pz)

    @pl.when(core == 0)
    def _():
        pz[0:OWN, :] = prev[:, wide]
        pz[OWN : 2 * OWN, :] = po[:, wide]

    @pl.when(core == 1)
    def _():
        pz[0:OWN, :] = po[:, wide]
        pz[OWN : 2 * OWN, :] = prev[:, wide]

    pzr[zl] = pz[...].astype(BF16)
    prev_l = [remote(pzr.at[zl], pzr.at[zl], l_s, l_r, d, dev_l[d]) for d in range(3)]
    for cp in prev_l:
        cp.start()

    for cp in loads:
        cp.wait()

    @pl.loop(0, T // 32)
    def _(i):
        rows = pl.ds(pl.multiple_of(i * 32, 32), 32)
        acc = jnp.zeros((32, 128), F32)
        for j in range(D // 128):
            v = tok[rows, j * 128 : (j + 1) * 128].astype(F32)
            acc = acc + v * v
        inv = lax.rsqrt(jnp.sum(acc, axis=-1, keepdims=True) * (1.0 / D) + eps)
        invb[rows, :] = jnp.broadcast_to(inv, (32, 128))

    def normed(b, put):
        @pl.loop(0, Q // 128)
        def _(j):
            rows = pl.ds(pl.multiple_of(j * 128, 128), 128)
            cols = tile(b, j)
            v = tok[:, cols].astype(F32) * invb[...] * gv[:, cols]
            put(rows, v.T.astype(BF16))

    def put_send(o):
        def put(rows, v):
            nst[o, rows, :] = v
        return put

    def put_own(o):
        def put(rows, v):
            nnt[o, rows, 0:T] = v
        return put

    send_n = []
    for o in range(2):
        normed(o, put_send(o))
        for p, start in enumerate((my_rows, its_rows)):
            rows = pl.ds(start, S)
            cp = remote(nst.at[o, rows], nnt.at[o, rows, pl.ds(T, T)], a_s, a_r, 1 + 2 * o + p, dev_a)
            cp.start()
            send_n.append(cp)

    for o in range(2):
        normed(2 + o, put_own(o))

    y_rows = pl.ds(pl.multiple_of(y * YR, 16), YR)
    prev_y = []

    def prev_to_y():
        for cp in prev_l:
            cp.wait_recv()
        for k in range(4):
            pa[k * 36 : (k + 1) * 36, :] = pzr[k, 0:36, :].astype(F32)
        pfull[core, y_rows, :] = pa[...].astype(BF16)
        prev_y.extend(
            [
                remote(pfull.at[core, y_rows], pfull.at[core, y_rows], y_s, y_r, d, dev_y[d])
                for d in range(3)
            ]
        )
        for cp in prev_y:
            cp.start()

    forward = [
        remote(
            wg.at[0, pl.ds(pl.multiple_of(my_rows + k * ZR, 16), ZR)],
            wg.at[0, pl.ds(pl.multiple_of(my_rows + k * ZR, 16), ZR)],
            b_s, b_r, 1 + k, dev_b,
        )
        for k in range(NZ)
    ]

    def pass_on(k):
        far_w[k].wait_recv()
        forward[k].start()

    def send_g(o, c):
        return remote(gs.at[o, c], gr.at[o, c], b_s, b_r, 5 + NC * o + c, dev_b)

    def product(o, rows, c):
        cols = pl.ds(pl.multiple_of(c * CW, 128), CW)
        return jnp.dot(nnt[o, pl.ds(rows, S), :], cc[:, cols], preferred_element_type=F32)

    def give(o):
        send_n[2 * o].wait_recv()

        @pl.loop(0, NC)
        def _(c):
            gs[o, c] = product(o, its_rows, c).astype(BF16)
            send_g(o, c).start()

    def keep(o):
        send_n[2 * o + 1].wait_recv()

        @pl.loop(0, NC)
        def _(c):
            gk[o, c] = product(o, my_rows, c)

    def send_s(c):
        return remote(zs.at[c], zr.at[c], z_s, z_r, NZ + c, dev_z)

    def far_sum(c):
        send_g(0, c).wait_recv()
        zs[c] = (gk[0, c] + gr[0, c].astype(F32)).astype(BF16)
        send_s(c).start()

    def dn(o, first, put):
        @pl.loop(0, 3)
        def _(n):
            rows = pl.ds(pl.multiple_of(n * 384, 128), 384)
            put(
                o,
                n * 384,
                lax.dot_general(
                    cc[first : first + T, :],
                    wg[o, rows, :],
                    (((1,), (1,)), ((), ())),
                    preferred_element_type=F32,
                ),
            )

    def put_xs(o, at, v):
        xs[:, pl.ds(pl.multiple_of(o * Q + at, 128), 384)] = v.astype(BF16)

    def put_xo(o, at, v):
        xa[:, pl.ds(pl.multiple_of(column(2 + o) + at, 128), 384)] = v.astype(BF16)

    own_plane = pl.ds(Q, Q)
    send_x1 = remote(
        xs.at[:, own_plane], xa.at[:, pl.ds(column(3), Q)], a_s, a_r, 5 + NT, dev_a
    )
    send_x = []
    for t in range(NT):
        rows = pl.ds(t * TR, TR)
        send_x.append(
            remote(xs.at[rows, pl.ds(0, Q)], xa.at[rows, pl.ds(column(2), Q)], a_s, a_r, 5 + t, dev_a)
        )

    def finish(t):
        send_x[t].wait_recv()

        @pl.loop(0, TR // 16)
        def _(i):
            rows = pl.ds(pl.multiple_of(t * TR + i * 16, 16), 16)
            inv = invb[rows, :]

            def parts(j):
                cols = slice(j * 128, (j + 1) * 128)
                unit = tok[rows, cols].astype(F32) * inv
                return unit, gv[:, cols] * xa[rows, cols].astype(F32)

            acc = jnp.zeros((16, 128), F32)
            for j in range(D // 128):
                unit, scaled = parts(j)
                acc = acc + unit * scaled
            mean = jnp.sum(acc, axis=-1, keepdims=True) * (1.0 / D)
            for j in range(D // 128):
                unit, scaled = parts(j)
                tok[rows, j * 128 : (j + 1) * 128] = (inv * (scaled - unit * mean)).astype(BF16)

    def send_up(c):
        return remote(up.at[2 * c + 1 - core], cr.at[c], c_s, c_r, 2 + c, dev_c)

    def send_y(c, d):
        rows = pl.ds(pl.multiple_of(lax.rem(y + d + 1, 4) * YR, 16), YR)
        return remote(s2.at[c, rows], yr.at[c, d], y_s, y_r, 3 + 3 * c + d, dev_y[d])

    def window(pos):
        return pl.multiple_of(pos * 36 - lax.rem(pos, 2) * 4, 8)

    def send_l(c, d):
        rows = pl.ds(window(lax.rem(zl + d + 1, 4)), WR)
        return remote(s8.at[c, rows], lr.at[c, d], l_s, l_r, 3 + 3 * c + d, dev_l[d])

    def send_tot(c):
        return remote(tot.at[2 * c + core], tot.at[2 * c + core], c_s, c_r, 6 + c, dev_c)

    def update(c):
        send_g(1, c).wait_recv()
        send_s(c).wait_recv()
        for k in range(2):
            part = slice(k * 128, (k + 1) * 128)
            cols = slice(c * CW + k * 128, c * CW + (k + 1) * 128)
            grad = gk[1, c, :, part] + gr[1, c, :, part].astype(F32) + zr[c, :, part].astype(F32)
            now = (wg[1, pl.ds(my_rows, S), cols].astype(F32) - inner_rate * grad).astype(BF16)
            up[2 * c + k] = now
        send_up(c).start()

    def mix(c):
        for k in range(2):
            cols = slice(c * CW + k * 128, c * CW + (k + 1) * 128)
            at = (c % 2) * CW + k * 128
            old = pfull[c // 2, :, at : at + 128].astype(F32)
            new_params[:, cols] = (
                (1.0 - mix_weight) * up[2 * c + k].astype(F32) + mix_weight * old
            ).astype(BF16)

    def both_cores(c):
        send_up(c).wait_recv()
        s2[c] = up[2 * c + core].astype(F32) + cr[c].astype(F32)
        for d in range(3):
            send_y(c, d).start()

    def all_y(c):
        for d in range(3):
            send_y(c, d).wait_recv()
        s8[c] = s2[c, y_rows, :] + yr[c, 0] + yr[c, 1] + yr[c, 2]
        for d in range(3):
            send_l(c, d).start()

    def all_l(c):
        for d in range(3):
            send_l(c, d).wait_recv()
        tot[2 * c + core] = s8[c, pl.ds(window(zl), WR), :] + lr[c, 0] + lr[c, 1] + lr[c, 2]
        send_tot(c).start()

    pass_on(0)
    pass_on(1)
    load_cot.wait()
    load_w.wait()
    send_cot.wait_recv()
    give(0)
    send_w.wait_recv()
    dn(1, T, put_xs)
    send_x1.start()
    pass_on(2)
    keep(0)
    far_sum(0)
    far_sum(1)
    pass_on(3)
    far_sum(2)
    give(1)
    far_sum(3)
    dn(1, 0, put_xo)
    keep(1)
    for cp in forward:
        cp.wait_recv()
    dn(0, T, put_xs)
    for cp in send_x:
        cp.start()
    dn(0, 0, put_xo)

    update(0)
    both_cores(0)
    update(1)
    all_y(0)
    both_cores(1)
    update(2)
    all_y(1)
    both_cores(2)
    send_x1.wait_recv()
    finish(0)
    all_y(2)
    finish(1)
    update(3)
    finish(2)
    both_cores(3)
    prev_to_y()
    finish(3)
    all_y(3)
    for cp in prev_y:
        cp.wait_recv()
    prev_c = remote(pfull.at[core], pfull.at[core], c_s, c_r, 1, dev_c)
    prev_c.start()
    all_l(0)
    all_l(1)
    all_l(2)
    finish(4)
    all_l(3)
    prev_c.wait_recv()
    for c in range(NC):
        mix(c)
    finish(5)

    for c in range(NC):
        send_tot(c).wait_recv()
    place = lax.rem(zl, 2) * 2 + core
    for j in range(HV // 128):
        cols = slice(j * 128, (j + 1) * 128)
        total = jnp.where(
            place < 2,
            jnp.where(place == 0, tot[j, 0:18, :], tot[j, 18:36, :]),
            jnp.where(place == 2, tot[j, 4:22, :], tot[j, 22:40, :]),
        )
        delta = glob[:, cols] - total * (1.0 / 32)
        moved = nesterov * mom[:, cols] + delta
        new_momentum[:, cols] = moved
        new_global[:, cols] = glob[:, cols] - outer_rate * (delta + nesterov * moved)
    finish(6)
    finish(7)

    for cp in [send_cot, send_w, send_prev, prev_c, send_x1] + far_w + forward + send_n + send_x + prev_l + prev_y:
        cp.wait_send()
    for c in range(NC):
        send_g(0, c).wait_send()
        send_g(1, c).wait_send()
        send_s(c).wait_send()
        send_up(c).wait_send()
        send_tot(c).wait_send()
        for d in range(3):
            send_y(c, d).wait_send()
            send_l(c, d).wait_send()


def store(n, *refs):
    sems = refs[-1]
    copies = [pltpu.make_async_copy(refs[i], refs[n + i], sems.at[i]) for i in range(n)]
    for cp in copies:
        cp.start()
    for cp in copies:
        cp.wait()


def shards(params, tokens, cotangent, gain, glob, momentum, prev_global):
    vmem = pl.BlockSpec(memory_space=pltpu.VMEM)
    hbm = pl.BlockSpec(memory_space=pl.ANY)
    dma = pltpu.SemaphoreType.DMA
    out = pl.pallas_call(
        kernel,
        out_shape=(
            pltpu.VMEM((S, HV), BF16),
            pltpu.VMEM((T, D), BF16),
            pltpu.VMEM((OWN, HV), F32),
            pltpu.VMEM((OWN, HV), F32),
        ),
        in_specs=[hbm, hbm, hbm, hbm, vmem, vmem, vmem],
        out_specs=(vmem, vmem, vmem, vmem),
        scratch_shapes=[
            pltpu.VMEM((2 * T, HV), BF16),
            pltpu.VMEM((T, 128), F32),
            pltpu.VMEM((1, D), F32),
            pltpu.VMEM((2, Q, T), BF16),
            pltpu.VMEM((2, Q, 2 * T), BF16),
            pltpu.VMEM((2, Q, HV), BF16),
            pltpu.VMEM((2, NC, S, CW), BF16),
            pltpu.VMEM((2, NC, S, CW), BF16),
            pltpu.VMEM((2, NC, S, CW), F32),
            pltpu.VMEM((NC, S, CW), BF16),
            pltpu.VMEM((NC, S, CW), BF16),
            pltpu.VMEM((2 * NC, S, 128), BF16),
            pltpu.VMEM((NC, S, 128), BF16),
            pltpu.VMEM((NC, S, 128), F32),
            pltpu.VMEM((NC, 3, YR, 128), F32),
            pltpu.VMEM((NC, YR, 128), F32),
            pltpu.VMEM((NC, 3, WR, 128), F32),
            pltpu.VMEM((2 * NC, WR, 128), F32),
            pltpu.VMEM((T, 2 * Q), BF16),
            pltpu.VMEM((T, D), BF16),
            pltpu.VMEM((OWN, HV), F32),
            pltpu.VMEM((PZ, HV // 2), F32),
            pltpu.VMEM((4, PZ, HV // 2), BF16),
            pltpu.VMEM((YR, HV // 2), F32),
            pltpu.VMEM((2, S, HV // 2), BF16),
            dma((6 + NT,)), dma((6 + NT,)),
            dma((5 + 2 * NC,)), dma((5 + 2 * NC,)),
            dma((NZ + NC,)), dma((NZ + NC,)),
            dma((2 + 2 * NC,)), dma((2 + 2 * NC,)),
            dma((3 + 3 * NC,)), dma((3 + 3 * NC,)),
            dma((3 + 3 * NC,)), dma((3 + 3 * NC,)),
            dma((4,)),
        ],
        compiler_params=pltpu.CompilerParams(
            collective_id=0, has_side_effects=True, vmem_limit_bytes=54 * 1024 * 1024
        ),
        cost_estimate=pl.CostEstimate(
            flops=4 * T * D * HV, bytes_accessed=16 * 1024 * 1024, transcendentals=T
        ),
        name="diloco",
    )(params[0], tokens[0], cotangent[0], gain, glob, momentum, prev_global)
    out = pl.pallas_call(
        functools.partial(store, len(out)),
        out_shape=tuple(jax.ShapeDtypeStruct(v.shape, v.dtype) for v in out),
        in_specs=[vmem] * len(out),
        out_specs=[hbm] * len(out),
        scratch_shapes=[dma((len(out),))],
        compiler_params=pltpu.CompilerParams(vmem_limit_bytes=1024 * 1024),
        name="store",
    )(*out)
    return (out[0][None], out[1][None], out[2], out[3])


def solution(mesh):
    placed = (
        P("replica", "fsdp", None),
        P("replica", "fsdp", None),
        P("replica", "fsdp", None),
        P(),
        P(("fsdp", "replica"), None),
        P(("fsdp", "replica"), None),
        P(("fsdp", "replica"), None),
    )
    return jax.shard_map(
        shards,
        mesh=mesh,
        in_specs=placed,
        out_specs=(
            P("replica", "fsdp", None),
            P("replica", "fsdp", None),
            P(("fsdp", "replica"), None),
            P(("fsdp", "replica"), None),
        ),
        check_vma=False,
    )
```

```python
import jax
import jax.numpy as jnp
from jax import lax
from jax.experimental import pallas as pl
from jax.experimental.pallas import tpu as pltpu
from jax.sharding import PartitionSpec as P

inner_rate = 0.5
outer_rate = 0.7
nesterov = 0.9
mix_weight = 0.5
eps = 1e-06

MESH = pl.DeviceIdType.MESH
F32 = jnp.float32
BF16 = jnp.bfloat16

D = 4608
HV = 1024
T = 512
Q = 1152
S = 576
NC = 4
CW = HV // NC
NT = 8
TR = T // NT
NZ = 4
ZR = S // NZ
YR = S // 4
WR = 24
OWN = 18
PZ = 48


def pieces(core):
    out = []
    for plane in (0, D // 2):
        out.append((plane, pl.multiple_of(plane + core * Q, 128), 512))
        out.append((plane + 512, pl.multiple_of(plane + (1 - core) * 512, 128), Q))
        out.append((plane + 512 + Q, plane + 512 + Q, Q - 512))
    return out


def kernel(
    params, tokens, cot, gain, glob, mom, prev,
    new_params, tok, new_global, new_momentum,
    cc, invb, gn, gv, nst, nnt, wg, gs, gr, gk, zs, zr, up, yr, s8, lr, tot,
    xs, xa, po, pz, pzr, pa, pfull,
    a_s, a_r, b_s, b_r, z_s, z_r, c_s, c_r, y_s, y_r, l_s, l_r, loc,
):
    rep = lax.axis_index("replica")
    fs = lax.axis_index("fsdp")
    core = lax.rem(rep, 2)
    zl = lax.rem(lax.div(rep, 2), 4)
    y = lax.div(rep, 8)
    x = lax.rem(fs, 4)
    zh = lax.div(fs, 4)
    half = jnp.where(core == 0, lax.div(x, 2), 1 - lax.rem(lax.div(x + 1, 2), 2))
    par = jnp.where(core == 0, lax.rem(x, 2), lax.div(x, 2))
    beside = x + 1 - 2 * lax.rem(x, 2)

    dev_a = (rep, zh * 4 + jnp.where(core == 0, 3 - x, beside))
    dev_b = (rep, zh * 4 + jnp.where(core == 0, beside, 3 - x))
    dev_z = (rep, (1 - zh) * 4 + x)
    dev_c = ((y * 4 + zl) * 2 + (1 - core), fs)

    def dev_y(i):
        return ((lax.rem(y + i // 2, 4) * 4 + zl) * 2 + lax.rem(core + i % 2, 2), fs)

    def dev_l(i):
        return ((y * 4 + lax.rem(zl + i // 2, 4)) * 2 + lax.rem(core + i % 2, 2), fs)

    def dev_zl(pos):
        return ((y * 4 + pos) * 2 + core, fs)

    def remote(src, dst, sends, recvs, i, dev):
        return pltpu.make_async_remote_copy(
            src_ref=src,
            dst_ref=dst,
            send_sem=sends.at[i],
            recv_sem=recvs.at[i],
            device_id=dev,
            device_id_type=MESH,
        )

    def column(b):
        plane = (1 - zh) if b % 2 == 0 else zh
        side = (1 - half) if b < 2 else half
        return pl.multiple_of(plane * (D // 2) + side * Q, 128)

    def tile(b, j):
        return pl.ds(pl.multiple_of(column(b) + j * 128, 128), 128)

    my_rows = pl.multiple_of(par * S, 64)
    its_rows = pl.multiple_of((1 - par) * S, 64)
    base = jnp.where((core == 1) & (half == 0), 64, 0)
    w_rows = pl.multiple_of(base + par * S, 64)

    def w_part(k):
        return pl.ds(pl.multiple_of(w_rows + k * ZR, 16), ZR)

    first_lanes = (lax.broadcasted_iota(jnp.int32, (16, 128), 1) < 64) & (core == 1)

    def exchange(v, u, mask):
        return jnp.where(mask, u, v), jnp.where(mask, v, u)

    loads = [
        pltpu.make_async_copy(
            tokens.at[:, pl.ds(start, width)], tok.at[:, pl.ds(place, width)], loc.at[4 + i]
        )
        for i, (start, place, width) in enumerate(pieces(core))
    ]
    loads.append(pltpu.make_async_copy(gain, gn.at[0], loc.at[1]))
    load_cot = pltpu.make_async_copy(cot, cc.at[pl.ds(0, T)], loc.at[2])
    load_w = pltpu.make_async_copy(params, wg.at[1, pl.ds(w_rows, S)], loc.at[3])

    barrier = pltpu.get_barrier_semaphore()
    peers = [dev_a, dev_b, dev_z] + [dev_y(i) for i in range(1, 8)] + [dev_l(i) for i in range(2, 8)]
    for dev in peers:
        pl.semaphore_signal(barrier, inc=1, device_id=dev, device_id_type=MESH)
    for cp in loads:
        cp.start()
    load_cot.start()
    load_w.start()
    pl.semaphore_wait(barrier, len(peers))

    send_prev = remote(prev, po, c_s, c_r, 0, dev_c)
    send_prev.start()
    send_cot = remote(cot, cc.at[pl.ds(T, T)], a_s, a_r, 0, dev_a)
    send_cot.start()
    send_w = remote(params, wg.at[1, pl.ds(w_rows, S)], b_s, b_r, 0, dev_b)
    send_w.start()
    far_w = [
        remote(
            params.at[pl.ds(k * ZR, ZR)],
            wg.at[0, w_part(k)],
            z_s, z_r, k, dev_z,
        )
        for k in range(NZ)
    ]
    far_w[0].start()

    send_prev.wait_recv()
    wide = pl.ds(pl.multiple_of(core * (HV // 2), 128), HV // 2)
    pz[...] = jnp.zeros_like(pz)

    @pl.when(core == 0)
    def _():
        pz[0:OWN, :] = prev[:, wide]
        pz[OWN : 2 * OWN, :] = po[:, wide]

    @pl.when(core == 1)
    def _():
        pz[0:OWN, :] = po[:, wide]
        pz[OWN : 2 * OWN, :] = prev[:, wide]

    pair, place_in = lax.div(zl, 2), lax.rem(zl, 2)
    edge = pair == place_in
    pzr[pair, place_in] = pz[...].astype(BF16)
    prev_l = remote(
        pzr.at[pair, place_in], pzr.at[pair, place_in], l_s, l_r, 0, dev_zl(zl + 1 - 2 * place_in)
    )
    prev_l.start()
    for cp in far_w[1:]:
        cp.start()

    relay = [
        pltpu.make_async_remote_copy(
            src_ref=pzr.at[pair],
            dst_ref=pzr.at[pair],
            send_sem=l_s.at[1 + k],
            recv_sem=l_r.at[1],
            device_id=dev_zl((1 - pair) * 2 + k),
            device_id_type=MESH,
        )
        for k in range(2)
    ]

    def pass_prev():
        prev_l.wait_recv()

        @pl.when(edge)
        def _():
            for cp in relay:
                cp.start()

    for cp in loads:
        cp.wait()
    for start, place, width in pieces(core):
        gv[:, pl.ds(place, width)] = gn[:, start : start + width]
    for plane in (0, D // 2):
        at, to = slice(plane, plane + 128), slice(plane + 512 + Q, plane + 640 + Q)
        gv[:, at], gv[:, to] = exchange(gv[:, at], gv[:, to], first_lanes[0:1, :])

        @pl.when(core == 1)
        def _():
            @pl.loop(0, T // 16)
            def _(i):
                rows = pl.ds(pl.multiple_of(i * 16, 16), 16)
                v, u = exchange(tok[rows, at].astype(F32), tok[rows, to].astype(F32), first_lanes)
                tok[rows, at] = v.astype(BF16)
                tok[rows, to] = u.astype(BF16)


    @pl.loop(0, T // 32)
    def _(i):
        rows = pl.ds(pl.multiple_of(i * 32, 32), 32)
        acc = jnp.zeros((32, 128), F32)
        for j in range(D // 128):
            v = tok[rows, j * 128 : (j + 1) * 128].astype(F32)
            acc = acc + v * v
        inv = lax.rsqrt(jnp.sum(acc, axis=-1, keepdims=True) * (1.0 / D) + eps)
        invb[rows, :] = jnp.broadcast_to(inv, (32, 128))

    def normed(b, put):
        @pl.loop(0, Q // 128)
        def _(j):
            cols = tile(b, j)
            v = (tok[:, cols].astype(F32) * invb[...] * gv[:, cols]).T.astype(BF16)
            side = (1 - half) if b < 2 else half
            shift = jnp.where((core == 1) & (side == 0), 64, 0)
            for k in range(2):
                row = lax.rem(j * 128 + k * 64 - shift + Q, Q)
                put(pl.ds(pl.multiple_of(row, 64), 64), v[k * 64 : (k + 1) * 64])

    def put_send(o):
        def put(rows, v):
            nst[o, rows, :] = v
        return put

    def put_own(o):
        def put(rows, v):
            nnt[o, rows, 0:T] = v
        return put

    send_n = []
    for o in range(2):
        normed(o, put_send(o))
        for p in range(2):
            rows = pl.ds(pl.multiple_of(jnp.where(core == p, my_rows, its_rows), 64), S)
            cp = remote(nst.at[o, rows], nnt.at[o, rows, pl.ds(T, T)], a_s, a_r, 1 + 2 * o + p, dev_a)
            cp.start()
            send_n.append(cp)

    for o in range(2):
        normed(2 + o, put_own(o))

    y_rows = pl.ds(pl.multiple_of(y * YR, 16), YR)
    prev_y = []

    def prev_to_y():
        relay[0].wait_recv()
        for k in range(4):
            pa[k * 36 : (k + 1) * 36, :] = pzr[k // 2, k % 2, 0:36, :].astype(F32)
        pfull[core, y_rows, :] = pa[...].astype(BF16)
        prev_y.extend(
            [
                remote(pfull.at[core, y_rows], pfull.at[core, y_rows], y_s, y_r, d, dev_y(2 * d + 2))
                for d in range(3)
            ]
        )
        for cp in prev_y:
            cp.start()

    forward = [
        remote(
            wg.at[0, w_part(k)],
            wg.at[0, w_part(k)],
            b_s, b_r, 1 + k, dev_b,
        )
        for k in range(NZ)
    ]

    def pass_on(k):
        far_w[k].wait_recv()
        forward[k].start()

    def send_g(o, c):
        return remote(gs.at[o, c], gr.at[o, c], b_s, b_r, 5 + NC * o + c, dev_b)

    def product(o, rows, c):
        cols = pl.ds(pl.multiple_of(c * CW, 128), CW)
        return jnp.dot(nnt[o, pl.ds(rows, S), :], cc[:, cols], preferred_element_type=F32)

    def give(o):
        send_n[2 * o].wait_recv()

        @pl.loop(0, NC)
        def _(c):
            gs[o, c] = product(o, its_rows, c).astype(BF16)
            send_g(o, c).start()

    def keep(o):
        send_n[2 * o + 1].wait_recv()

        @pl.loop(0, NC)
        def _(c):
            gk[o, c] = product(o, my_rows, c)

    def send_s(c):
        return remote(zs.at[c], zr.at[c], z_s, z_r, NZ + c, dev_z)

    def far_sum(c):
        send_g(0, c).wait_recv()
        zs[c] = (gk[0, c] + gr[0, c].astype(F32)).astype(BF16)
        send_s(c).start()

    def wrap(o):
        @pl.when(base == 64)
        def _():
            wg[o, 0:64, :] = wg[o, Q : Q + 64, :]

    def dn(o, first, put):
        @pl.loop(0, 3)
        def _(n):
            rows = pl.ds(pl.multiple_of(n * 384, 128), 384)
            put(
                o,
                n * 384,
                lax.dot_general(
                    cc[first : first + T, :],
                    wg[o, rows, :],
                    (((1,), (1,)), ((), ())),
                    preferred_element_type=F32,
                ),
            )

    def put_xs(o, at, v):
        xs[:, pl.ds(pl.multiple_of(o * Q + at, 128), 384)] = v.astype(BF16)

    def put_xo(o, at, v):
        xa[:, pl.ds(pl.multiple_of(column(2 + o) + at, 128), 384)] = v.astype(BF16)

    own_plane = pl.ds(Q, Q)
    send_x1 = remote(
        xs.at[:, own_plane], xa.at[:, pl.ds(column(3), Q)], a_s, a_r, 5 + NT, dev_a
    )
    send_x = []
    for t in range(NT):
        rows = pl.ds(t * TR, TR)
        send_x.append(
            remote(xs.at[rows, pl.ds(0, Q)], xa.at[rows, pl.ds(column(2), Q)], a_s, a_r, 5 + t, dev_a)
        )

    def finish(t):
        send_x[t].wait_recv()

        @pl.loop(0, TR // 16)
        def _(i):
            rows = pl.ds(pl.multiple_of(t * TR + i * 16, 16), 16)
            inv = invb[rows, :]

            def parts(j):
                cols = slice(j * 128, (j + 1) * 128)
                unit = tok[rows, cols].astype(F32) * inv
                return unit, gv[:, cols] * xa[rows, cols].astype(F32)

            acc = jnp.zeros((16, 128), F32)
            for j in range(D // 128):
                unit, scaled = parts(j)
                acc = acc + unit * scaled
            mean = jnp.sum(acc, axis=-1, keepdims=True) * (1.0 / D)

            def result(j):
                unit, scaled = parts(j)
                return inv * (scaled - unit * mean)

            def put(j, v):
                tok[rows, j * 128 : (j + 1) * 128] = v.astype(BF16)

            for plane in (0, D // 256):
                last = plane + (512 + Q) // 128
                v, u = exchange(result(plane), result(last), first_lanes)
                put(plane, v)
                put(last, u)
                for j in range(plane + 1, plane + D // 256):
                    if j != last:
                        put(j, result(j))

    def send_y(c, i):
        rows = pl.ds(pl.multiple_of(lax.rem(y + i // 2, 4) * YR, 16), YR)
        src = up.at[2 * c + lax.rem(core + i % 2, 2), rows]
        return remote(src, yr.at[c, i], y_s, y_r, 2 + 7 * c + i, dev_y(i))

    def window(pos):
        return pl.ds(pl.multiple_of(lax.div(pos * OWN, 8) * 8, 8), WR)

    def send_l(c, i):
        pos = lax.rem(zl + i // 2, 4) * 2 + lax.rem(core + i % 2, 2)
        return remote(s8.at[c, window(pos)], lr.at[c, i], l_s, l_r, 2 + 7 * c + i, dev_l(i))

    def update(c):
        send_g(1, c).wait_recv()
        send_s(c).wait_recv()
        for k in range(2):
            part = slice(k * 128, (k + 1) * 128)
            cols = slice(c * CW + k * 128, c * CW + (k + 1) * 128)
            grad = gk[1, c, :, part] + gr[1, c, :, part].astype(F32) + zr[c, :, part].astype(F32)
            now = (wg[1, pl.ds(w_rows, S), cols].astype(F32) - inner_rate * grad).astype(BF16)
            up[2 * c + k] = now
        for i in range(1, 8):
            send_y(c, i).start()

    def mix(c):
        for k in range(2):
            cols = slice(c * CW + k * 128, c * CW + (k + 1) * 128)
            at = (c % 2) * CW + k * 128
            old = pfull[c // 2, :, at : at + 128].astype(F32)
            new_params[:, cols] = (
                (1.0 - mix_weight) * up[2 * c + k].astype(F32) + mix_weight * old
            ).astype(BF16)

    def all_y(c):
        for i in range(1, 8):
            send_y(c, i).wait_recv()
        total = up[2 * c + core, y_rows, :].astype(F32)
        for i in range(1, 8):
            total = total + yr[c, i].astype(F32)
        s8[c] = total
        for i in range(1, 8):
            send_l(c, i).start()

    def all_l(c):
        for i in range(1, 8):
            send_l(c, i).wait_recv()
        tot[2 * c + core] = s8[c, window(zl * 2 + core), :] + lr[c, 2] + lr[c, 4] + lr[c, 6]
        tot[2 * c + 1 - core] = lr[c, 1] + lr[c, 3] + lr[c, 5] + lr[c, 7]

    pass_on(0)
    pass_on(1)
    pass_prev()
    load_cot.wait()
    load_w.wait()
    send_cot.wait_recv()
    give(0)
    send_w.wait_recv()
    wrap(1)
    dn(1, T, put_xs)
    send_x1.start()
    pass_on(2)
    keep(0)
    far_sum(0)
    far_sum(1)
    pass_on(3)
    far_sum(2)
    give(1)
    far_sum(3)
    dn(1, 0, put_xo)
    keep(1)
    for cp in forward:
        cp.wait_recv()
    wrap(0)
    dn(0, T, put_xs)
    for cp in send_x:
        cp.start()
    dn(0, 0, put_xo)

    update(0)
    prev_to_y()
    update(1)
    for cp in prev_y:
        cp.wait_recv()
    prev_c = remote(pfull.at[core], pfull.at[core], c_s, c_r, 1, dev_c)
    prev_c.start()
    all_y(0)
    update(2)
    prev_c.wait_recv()
    mix(0)
    mix(1)
    all_y(1)
    send_x1.wait_recv()
    finish(0)
    mix(2)
    all_y(2)
    finish(1)
    update(3)
    mix(3)
    finish(2)
    finish(3)
    finish(4)
    all_y(3)
    all_l(0)
    all_l(1)
    all_l(2)
    finish(5)
    finish(6)
    all_l(3)

    place = lax.rem(zl, 2) * 2 + core
    for j in range(HV // 128):
        cols = slice(j * 128, (j + 1) * 128)
        total = jnp.where(
            place < 2,
            jnp.where(place == 0, tot[j, 0:18, :], tot[j, 2:20, :]),
            jnp.where(place == 2, tot[j, 4:22, :], tot[j, 6:24, :]),
        )
        delta = glob[:, cols] - total * (1.0 / 32)
        moved = nesterov * mom[:, cols] + delta
        new_momentum[:, cols] = moved
        new_global[:, cols] = glob[:, cols] - outer_rate * (delta + nesterov * moved)
    finish(7)

    for cp in [send_cot, send_w, send_prev, prev_c, send_x1, prev_l] + far_w + forward + send_n + send_x + prev_y:
        cp.wait_send()

    @pl.when(edge)
    def _():
        for cp in relay:
            cp.wait_send()

    for c in range(NC):
        send_g(0, c).wait_send()
        send_g(1, c).wait_send()
        send_s(c).wait_send()
        for i in range(1, 8):
            send_y(c, i).wait_send()
            send_l(c, i).wait_send()


def store(params, tok, glob, mom, params_out, tokens_out, glob_out, mom_out, sems):
    core = lax.rem(lax.axis_index("replica"), 2)
    copies = [
        pltpu.make_async_copy(
            tok.at[:, pl.ds(place, width)], tokens_out.at[:, pl.ds(start, width)], sems.at[i]
        )
        for i, (start, place, width) in enumerate(pieces(core))
    ]
    n = len(copies)
    for i, (src, dst) in enumerate(((params, params_out), (glob, glob_out), (mom, mom_out))):
        copies.append(pltpu.make_async_copy(src, dst, sems.at[n + i]))
    for cp in copies:
        cp.start()
    for cp in copies:
        cp.wait()


def shards(params, tokens, cotangent, gain, glob, momentum, prev_global):
    vmem = pl.BlockSpec(memory_space=pltpu.VMEM)
    hbm = pl.BlockSpec(memory_space=pl.ANY)
    dma = pltpu.SemaphoreType.DMA
    out = pl.pallas_call(
        kernel,
        out_shape=(
            pltpu.VMEM((S, HV), BF16),
            pltpu.VMEM((T, D), BF16),
            pltpu.VMEM((OWN, HV), F32),
            pltpu.VMEM((OWN, HV), F32),
        ),
        in_specs=[hbm, hbm, hbm, hbm, vmem, vmem, vmem],
        out_specs=(vmem, vmem, vmem, vmem),
        scratch_shapes=[
            pltpu.VMEM((2 * T, HV), BF16),
            pltpu.VMEM((T, 128), F32),
            pltpu.VMEM((1, D), F32),
            pltpu.VMEM((1, D), F32),
            pltpu.VMEM((2, Q, T), BF16),
            pltpu.VMEM((2, Q, 2 * T), BF16),
            pltpu.VMEM((2, Q + 64, HV), BF16),
            pltpu.VMEM((2, NC, S, CW), BF16),
            pltpu.VMEM((2, NC, S, CW), BF16),
            pltpu.VMEM((2, NC, S, CW), F32),
            pltpu.VMEM((NC, S, CW), BF16),
            pltpu.VMEM((NC, S, CW), BF16),
            pltpu.VMEM((2 * NC, S, 128), BF16),
            pltpu.VMEM((NC, 8, YR, 128), BF16),
            pltpu.VMEM((NC, YR, 128), F32),
            pltpu.VMEM((NC, 8, WR, 128), F32),
            pltpu.VMEM((2 * NC, WR, 128), F32),
            pltpu.VMEM((T, 2 * Q), BF16),
            pltpu.VMEM((T, D), BF16),
            pltpu.VMEM((OWN, HV), F32),
            pltpu.VMEM((PZ, HV // 2), F32),
            pltpu.VMEM((2, 2, PZ, HV // 2), BF16),
            pltpu.VMEM((YR, HV // 2), F32),
            pltpu.VMEM((2, S, HV // 2), BF16),
            dma((6 + NT,)), dma((6 + NT,)),
            dma((5 + 2 * NC,)), dma((5 + 2 * NC,)),
            dma((NZ + NC,)), dma((NZ + NC,)),
            dma((2,)), dma((2,)),
            dma((3 + 7 * NC,)), dma((3 + 7 * NC,)),
            dma((3 + 7 * NC,)), dma((3 + 7 * NC,)),
            dma((10,)),
        ],
        compiler_params=pltpu.CompilerParams(
            collective_id=0, has_side_effects=True, vmem_limit_bytes=54 * 1024 * 1024
        ),
        cost_estimate=pl.CostEstimate(
            flops=4 * T * D * HV, bytes_accessed=16 * 1024 * 1024, transcendentals=T
        ),
        name="diloco",
    )(params[0], tokens[0], cotangent[0], gain, glob, momentum, prev_global)
    out = pl.pallas_call(
        store,
        out_shape=tuple(jax.ShapeDtypeStruct(v.shape, v.dtype) for v in out),
        in_specs=[vmem] * len(out),
        out_specs=[hbm] * len(out),
        scratch_shapes=[dma((9,))],
        compiler_params=pltpu.CompilerParams(vmem_limit_bytes=1024 * 1024),
        name="store",
    )(*out)
    return (out[0][None], out[1][None], out[2], out[3])


def solution(mesh):
    placed = (
        P("replica", "fsdp", None),
        P("replica", "fsdp", None),
        P("replica", "fsdp", None),
        P(),
        P(("fsdp", "replica"), None),
        P(("fsdp", "replica"), None),
        P(("fsdp", "replica"), None),
    )
    return jax.shard_map(
        shards,
        mesh=mesh,
        in_specs=placed,
        out_specs=(
            P("replica", "fsdp", None),
            P("replica", "fsdp", None),
            P(("fsdp", "replica"), None),
            P(("fsdp", "replica"), None),
        ),
        check_vma=False,
    )
```

```python
import jax
import jax.numpy as jnp
from jax import lax
from jax.experimental import pallas as pl
from jax.experimental.pallas import tpu as pltpu
from jax.sharding import PartitionSpec as P

inner_rate = 0.5
outer_rate = 0.7
nesterov = 0.9
mix_weight = 0.5
eps = 1e-06

MESH = pl.DeviceIdType.MESH
F32 = jnp.float32
BF16 = jnp.bfloat16

D = 4608
HV = 1024
T = 512
Q = 1152
S = 576
NC = 4
CW = HV // NC
NT = 8
TR = T // NT
NZ = 4
ZR = S // NZ
YR = S // 4
WR = 24
OWN = 18
PZ = 48


def pieces(core):
    out = []
    for plane in (0, D // 2):
        out.append((plane, pl.multiple_of(plane + core * Q, 128), 512))
        out.append((plane + 512, pl.multiple_of(plane + (1 - core) * 512, 128), Q))
        out.append((plane + 512 + Q, plane + 512 + Q, Q - 512))
    return out


def kernel(
    params, tokens, cot, gain, glob, mom, prev,
    new_params, tok, new_global, new_momentum,
    cc, invb, gn, gv, nst, nnt, wg, gs, gr, gk, zs, zr, up, yr, s8, lr, tot,
    xs, xa, po, pz, pzr, pa, pfull,
    a_s, a_r, b_s, b_r, z_s, z_r, c_s, c_r, y_s, y_r, l_s, l_r, loc,
):
    rep = lax.axis_index("replica")
    fs = lax.axis_index("fsdp")
    core = lax.rem(rep, 2)
    zl = lax.rem(lax.div(rep, 2), 4)
    y = lax.div(rep, 8)
    x = lax.rem(fs, 4)
    zh = lax.div(fs, 4)
    half = jnp.where(core == 0, lax.div(x, 2), 1 - lax.rem(lax.div(x + 1, 2), 2))
    par = jnp.where(core == 0, lax.rem(x, 2), lax.div(x, 2))
    beside = x + 1 - 2 * lax.rem(x, 2)

    dev_a = (rep, zh * 4 + jnp.where(core == 0, 3 - x, beside))
    dev_b = (rep, zh * 4 + jnp.where(core == 0, beside, 3 - x))
    dev_z = (rep, (1 - zh) * 4 + x)
    dev_c = ((y * 4 + zl) * 2 + (1 - core), fs)

    def dev_y(i):
        return ((lax.rem(y + i // 2, 4) * 4 + zl) * 2 + lax.rem(core + i % 2, 2), fs)

    def dev_l(i):
        return ((y * 4 + lax.rem(zl + i // 2, 4)) * 2 + lax.rem(core + i % 2, 2), fs)

    def dev_zl(pos):
        return ((y * 4 + pos) * 2 + core, fs)

    def remote(src, dst, sends, recvs, i, dev):
        return pltpu.make_async_remote_copy(
            src_ref=src,
            dst_ref=dst,
            send_sem=sends.at[i],
            recv_sem=recvs.at[i],
            device_id=dev,
            device_id_type=MESH,
        )

    def column(b):
        plane = (1 - zh) if b % 2 == 0 else zh
        side = (1 - half) if b < 2 else half
        return pl.multiple_of(plane * (D // 2) + side * Q, 128)

    def tile(b, j):
        return pl.ds(pl.multiple_of(column(b) + j * 128, 128), 128)

    my_rows = pl.multiple_of(par * S, 64)
    its_rows = pl.multiple_of((1 - par) * S, 64)
    base = jnp.where((core == 1) & (half == 0), 64, 0)
    w_rows = pl.multiple_of(base + par * S, 64)

    def w_part(k):
        return pl.ds(pl.multiple_of(w_rows + k * ZR, 16), ZR)

    first_lanes = (lax.broadcasted_iota(jnp.int32, (16, 128), 1) < 64) & (core == 1)

    def exchange(v, u, mask):
        return jnp.where(mask, u, v), jnp.where(mask, v, u)

    loads = [
        pltpu.make_async_copy(
            tokens.at[:, pl.ds(start, width)], tok.at[:, pl.ds(place, width)], loc.at[4 + i]
        )
        for i, (start, place, width) in enumerate(pieces(core))
    ]
    loads.append(pltpu.make_async_copy(gain, gn.at[0], loc.at[1]))
    load_cot = pltpu.make_async_copy(cot, cc.at[pl.ds(0, T)], loc.at[2])
    load_w = pltpu.make_async_copy(params, wg.at[1, pl.ds(w_rows, S)], loc.at[3])

    barrier = pltpu.get_barrier_semaphore()
    peers = [dev_a, dev_b, dev_z] + [dev_y(i) for i in range(1, 8)] + [dev_l(i) for i in range(2, 8)]
    for dev in peers:
        pl.semaphore_signal(barrier, inc=1, device_id=dev, device_id_type=MESH)
    for cp in loads:
        cp.start()
    load_cot.start()
    load_w.start()
    pl.semaphore_wait(barrier, len(peers))

    send_prev = remote(prev, po, c_s, c_r, 0, dev_c)
    send_prev.start()
    send_cot = remote(cot, cc.at[pl.ds(T, T)], a_s, a_r, 0, dev_a)
    send_cot.start()
    send_w = remote(params, wg.at[1, pl.ds(w_rows, S)], b_s, b_r, 0, dev_b)
    send_w.start()
    far_w = [
        remote(
            params.at[pl.ds(k * ZR, ZR)],
            wg.at[0, w_part(k)],
            z_s, z_r, k, dev_z,
        )
        for k in range(NZ)
    ]
    far_w[0].start()

    send_prev.wait_recv()
    wide = pl.ds(pl.multiple_of(core * (HV // 2), 128), HV // 2)
    pz[...] = jnp.zeros_like(pz)

    @pl.when(core == 0)
    def _():
        pz[0:OWN, :] = prev[:, wide]
        pz[OWN : 2 * OWN, :] = po[:, wide]

    @pl.when(core == 1)
    def _():
        pz[0:OWN, :] = po[:, wide]
        pz[OWN : 2 * OWN, :] = prev[:, wide]

    pair, place_in = lax.div(zl, 2), lax.rem(zl, 2)
    edge = pair == place_in
    pzr[pair, place_in] = pz[...].astype(BF16)
    prev_l = remote(
        pzr.at[pair, place_in], pzr.at[pair, place_in], l_s, l_r, 0, dev_zl(zl + 1 - 2 * place_in)
    )
    prev_l.start()
    for cp in far_w[1:]:
        cp.start()

    relay = [
        pltpu.make_async_remote_copy(
            src_ref=pzr.at[pair],
            dst_ref=pzr.at[pair],
            send_sem=l_s.at[1 + k],
            recv_sem=l_r.at[1],
            device_id=dev_zl((1 - pair) * 2 + k),
            device_id_type=MESH,
        )
        for k in range(2)
    ]

    def pass_prev():
        prev_l.wait_recv()

        @pl.when(edge)
        def _():
            for cp in relay:
                cp.start()

    for cp in loads:
        cp.wait()
    for start, place, width in pieces(core):
        gv[:, pl.ds(place, width)] = gn[:, start : start + width]
    for plane in (0, D // 2):
        at, to = slice(plane, plane + 128), slice(plane + 512 + Q, plane + 640 + Q)
        gv[:, at], gv[:, to] = exchange(gv[:, at], gv[:, to], first_lanes[0:1, :])

        @pl.when(core == 1)
        def _():
            @pl.loop(0, T // 16)
            def _(i):
                rows = pl.ds(pl.multiple_of(i * 16, 16), 16)
                v, u = exchange(tok[rows, at].astype(F32), tok[rows, to].astype(F32), first_lanes)
                tok[rows, at] = v.astype(BF16)
                tok[rows, to] = u.astype(BF16)


    @pl.loop(0, T // 32)
    def _(i):
        rows = pl.ds(pl.multiple_of(i * 32, 32), 32)
        acc = jnp.zeros((32, 128), F32)
        for j in range(D // 128):
            v = tok[rows, j * 128 : (j + 1) * 128].astype(F32)
            acc = acc + v * v
        inv = lax.rsqrt(jnp.sum(acc, axis=-1, keepdims=True) * (1.0 / D) + eps)
        invb[rows, :] = jnp.broadcast_to(inv, (32, 128))

    def normed(b, put):
        @pl.loop(0, Q // 128)
        def _(j):
            cols = tile(b, j)
            v = (tok[:, cols].astype(F32) * invb[...] * gv[:, cols]).T.astype(BF16)
            side = (1 - half) if b < 2 else half
            shift = jnp.where((core == 1) & (side == 0), 64, 0)
            for k in range(2):
                row = lax.rem(j * 128 + k * 64 - shift + Q, Q)
                put(pl.ds(pl.multiple_of(row, 64), 64), v[k * 64 : (k + 1) * 64])

    def put_send(o):
        def put(rows, v):
            nst[o, rows, :] = v
        return put

    def put_own(o):
        def put(rows, v):
            nnt[o, rows, 0:T] = v
        return put

    send_n = []
    for o in range(2):
        normed(o, put_send(o))
        for p in range(2):
            rows = pl.ds(pl.multiple_of(jnp.where(core == p, my_rows, its_rows), 64), S)
            cp = remote(nst.at[o, rows], nnt.at[o, rows, pl.ds(T, T)], a_s, a_r, 1 + 2 * o + p, dev_a)
            cp.start()
            send_n.append(cp)

    for o in range(2):
        normed(2 + o, put_own(o))

    y_rows = pl.ds(pl.multiple_of(y * YR, 16), YR)
    prev_y = []

    def prev_to_y():
        relay[0].wait_recv()
        for k in range(4):
            pa[k * 36 : (k + 1) * 36, :] = pzr[k // 2, k % 2, 0:36, :].astype(F32)
        pfull[core, y_rows, :] = pa[...].astype(BF16)
        prev_y.extend(
            [
                remote(pfull.at[core, y_rows], pfull.at[core, y_rows], y_s, y_r, d, dev_y(2 * d + 2))
                for d in range(3)
            ]
        )
        for cp in prev_y:
            cp.start()

    forward = [
        remote(
            wg.at[0, w_part(k)],
            wg.at[0, w_part(k)],
            b_s, b_r, 1 + k, dev_b,
        )
        for k in range(NZ)
    ]

    def pass_on(k):
        far_w[k].wait_recv()
        forward[k].start()

    def send_g(o, c):
        return remote(gs.at[o, c], gr.at[o, c], b_s, b_r, 5 + NC * o + c, dev_b)

    def product(o, rows, c):
        cols = pl.ds(pl.multiple_of(c * CW, 128), CW)
        return jnp.dot(nnt[o, pl.ds(rows, S), :], cc[:, cols], preferred_element_type=F32)

    def give(o):
        send_n[2 * o].wait_recv()

        @pl.loop(0, NC)
        def _(c):
            gs[o, c] = product(o, its_rows, c).astype(BF16)
            send_g(o, c).start()

    def keep(o):
        send_n[2 * o + 1].wait_recv()

        @pl.loop(0, NC)
        def _(c):
            gk[o, c] = product(o, my_rows, c)

    def send_s(c):
        return remote(zs.at[c], zr.at[c], z_s, z_r, NZ + c, dev_z)

    def far_sum(c):
        send_g(0, c).wait_recv()
        zs[c] = (gk[0, c] + gr[0, c].astype(F32)).astype(BF16)
        send_s(c).start()

    def wrap(o):
        @pl.when(base == 64)
        def _():
            wg[o, 0:64, :] = wg[o, Q : Q + 64, :]

    def dn(o, first, put):
        @pl.loop(0, 3)
        def _(n):
            rows = pl.ds(pl.multiple_of(n * 384, 128), 384)
            put(
                o,
                n * 384,
                lax.dot_general(
                    cc[first : first + T, :],
                    wg[o, rows, :],
                    (((1,), (1,)), ((), ())),
                    preferred_element_type=F32,
                ),
            )

    def put_xs(o, at, v):
        xs[:, pl.ds(pl.multiple_of(o * Q + at, 128), 384)] = v.astype(BF16)

    def put_xo(o, at, v):
        xa[:, pl.ds(pl.multiple_of(column(2 + o) + at, 128), 384)] = v.astype(BF16)

    own_plane = pl.ds(Q, Q)
    send_x1 = remote(
        xs.at[:, own_plane], xa.at[:, pl.ds(column(3), Q)], a_s, a_r, 5 + NT, dev_a
    )
    send_x = []
    for t in range(NT):
        rows = pl.ds(t * TR, TR)
        send_x.append(
            remote(xs.at[rows, pl.ds(0, Q)], xa.at[rows, pl.ds(column(2), Q)], a_s, a_r, 5 + t, dev_a)
        )

    def finish(t):
        send_x[t].wait_recv()

        @pl.loop(0, TR // 16)
        def _(i):
            rows = pl.ds(pl.multiple_of(t * TR + i * 16, 16), 16)
            inv = invb[rows, :]

            def parts(j):
                cols = slice(j * 128, (j + 1) * 128)
                unit = tok[rows, cols].astype(F32) * inv
                return unit, gv[:, cols] * xa[rows, cols].astype(F32)

            acc = jnp.zeros((16, 128), F32)
            for j in range(D // 128):
                unit, scaled = parts(j)
                acc = acc + unit * scaled
            mean = jnp.sum(acc, axis=-1, keepdims=True) * (1.0 / D)

            def result(j):
                unit, scaled = parts(j)
                return inv * (scaled - unit * mean)

            def put(j, v):
                tok[rows, j * 128 : (j + 1) * 128] = v.astype(BF16)

            for plane in (0, D // 256):
                last = plane + (512 + Q) // 128
                v, u = exchange(result(plane), result(last), first_lanes)
                put(plane, v)
                put(last, u)
                for j in range(plane + 1, plane + D // 256):
                    if j != last:
                        put(j, result(j))

    def send_y(c, i):
        rows = pl.ds(pl.multiple_of(lax.rem(y + i // 2, 4) * YR, 16), YR)
        src = up.at[2 * c + lax.rem(core + i % 2, 2), rows]
        return remote(src, yr.at[c, i], y_s, y_r, 2 + 7 * c + i, dev_y(i))

    def window(pos):
        return pl.ds(pl.multiple_of(lax.div(pos * OWN, 8) * 8, 8), WR)

    def send_l(first, count, i):
        pos = lax.rem(zl + i // 2, 4) * 2 + lax.rem(core + i % 2, 2)
        chunks = pl.ds(first, count)
        sem = 2 + i + (7 if first else 0)
        return remote(s8.at[chunks, window(pos)], lr.at[chunks, i], l_s, l_r, sem, dev_l(i))

    def update(c):
        send_g(1, c).wait_recv()
        send_s(c).wait_recv()
        for k in range(2):
            part = slice(k * 128, (k + 1) * 128)
            cols = slice(c * CW + k * 128, c * CW + (k + 1) * 128)
            grad = gk[1, c, :, part] + gr[1, c, :, part].astype(F32) + zr[c, :, part].astype(F32)
            now = (wg[1, pl.ds(w_rows, S), cols].astype(F32) - inner_rate * grad).astype(BF16)
            up[2 * c + k] = now
        for i in (4, 5, 2, 3, 6, 7, 1):
            send_y(c, i).start()

    def mix(c):
        for k in range(2):
            cols = slice(c * CW + k * 128, c * CW + (k + 1) * 128)
            at = (c % 2) * CW + k * 128
            old = pfull[c // 2, :, at : at + 128].astype(F32)
            new_params[:, cols] = (
                (1.0 - mix_weight) * up[2 * c + k].astype(F32) + mix_weight * old
            ).astype(BF16)

    def all_y(c):
        for i in range(1, 8):
            send_y(c, i).wait_recv()
        total = up[2 * c + core, y_rows, :].astype(F32)
        for i in range(1, 8):
            total = total + yr[c, i].astype(F32)
        s8[c] = total

    far_first = (4, 5, 2, 3, 6, 7, 1)

    def start_l(first, count):
        for i in far_first:
            send_l(first, count, i).start()

    def all_l(first, count):
        for i in range(1, 8):
            send_l(first, count, i).wait_recv()
        for c in range(first, first + count):
            tot[2 * c + core] = s8[c, window(zl * 2 + core), :] + lr[c, 2] + lr[c, 4] + lr[c, 6]
            tot[2 * c + 1 - core] = lr[c, 1] + lr[c, 3] + lr[c, 5] + lr[c, 7]

    def sent(*copies):
        for cp in copies:
            cp.wait_send()

    pass_on(0)
    pass_on(1)
    pass_prev()
    load_cot.wait()
    load_w.wait()
    send_cot.wait_recv()
    give(0)
    send_w.wait_recv()
    wrap(1)
    dn(1, T, put_xs)
    send_x1.start()
    pass_on(2)
    keep(0)
    far_sum(0)
    far_sum(1)
    pass_on(3)
    far_sum(2)
    give(1)
    far_sum(3)
    dn(1, 0, put_xo)
    sent(send_cot, send_w, send_prev, prev_l, *far_w, *send_n[:3])
    keep(1)
    for cp in forward:
        cp.wait_recv()
    wrap(0)
    dn(0, T, put_xs)
    for cp in send_x:
        cp.start()
    dn(0, 0, put_xo)
    sent(send_n[3], *forward, *[send_g(0, c) for c in range(NC)])

    @pl.when(edge)
    def _():
        sent(*relay)

    update(0)
    prev_to_y()
    update(1)
    for cp in prev_y:
        cp.wait_recv()
    prev_c = remote(pfull.at[core], pfull.at[core], c_s, c_r, 1, dev_c)
    prev_c.start()
    all_y(0)
    update(2)
    prev_c.wait_recv()
    mix(0)
    mix(1)
    all_y(1)
    send_x1.wait_recv()
    finish(0)
    mix(2)
    finish(1)
    finish(2)
    sent(prev_c, send_x1, *prev_y, *[send_g(1, c) for c in range(NC)])
    update(3)
    all_y(2)
    start_l(0, 3)
    finish(3)
    finish(4)
    finish(5)
    all_y(3)
    start_l(3, 1)
    mix(3)
    finish(6)
    finish(7)
    sent(*send_x, *[send_s(c) for c in range(NC)], *[send_y(c, i) for c in range(NC) for i in range(1, 8)])
    all_l(0, 3)
    all_l(3, 1)

    place = lax.rem(zl, 2) * 2 + core
    for j in range(HV // 128):
        cols = slice(j * 128, (j + 1) * 128)
        total = jnp.where(
            place < 2,
            jnp.where(place == 0, tot[j, 0:18, :], tot[j, 2:20, :]),
            jnp.where(place == 2, tot[j, 4:22, :], tot[j, 6:24, :]),
        )
        delta = glob[:, cols] - total * (1.0 / 32)
        moved = nesterov * mom[:, cols] + delta
        new_momentum[:, cols] = moved
        new_global[:, cols] = glob[:, cols] - outer_rate * (delta + nesterov * moved)

    sent(*[send_l(first, count, i) for first, count in ((0, 3), (3, 1)) for i in range(1, 8)])


def store(params, tok, glob, mom, params_out, tokens_out, glob_out, mom_out, sems):
    core = lax.rem(lax.axis_index("replica"), 2)
    copies = [
        pltpu.make_async_copy(
            tok.at[:, pl.ds(place, width)], tokens_out.at[:, pl.ds(start, width)], sems.at[i]
        )
        for i, (start, place, width) in enumerate(pieces(core))
    ]
    n = len(copies)
    for i, (src, dst) in enumerate(((params, params_out), (glob, glob_out), (mom, mom_out))):
        copies.append(pltpu.make_async_copy(src, dst, sems.at[n + i]))
    for cp in copies:
        cp.start()
    for cp in copies:
        cp.wait()


def shards(params, tokens, cotangent, gain, glob, momentum, prev_global):
    vmem = pl.BlockSpec(memory_space=pltpu.VMEM)
    hbm = pl.BlockSpec(memory_space=pl.ANY)
    dma = pltpu.SemaphoreType.DMA
    out = pl.pallas_call(
        kernel,
        out_shape=(
            pltpu.VMEM((S, HV), BF16),
            pltpu.VMEM((T, D), BF16),
            pltpu.VMEM((OWN, HV), F32),
            pltpu.VMEM((OWN, HV), F32),
        ),
        in_specs=[hbm, hbm, hbm, hbm, vmem, vmem, vmem],
        out_specs=(vmem, vmem, vmem, vmem),
        scratch_shapes=[
            pltpu.VMEM((2 * T, HV), BF16),
            pltpu.VMEM((T, 128), F32),
            pltpu.VMEM((1, D), F32),
            pltpu.VMEM((1, D), F32),
            pltpu.VMEM((2, Q, T), BF16),
            pltpu.VMEM((2, Q, 2 * T), BF16),
            pltpu.VMEM((2, Q + 64, HV), BF16),
            pltpu.VMEM((2, NC, S, CW), BF16),
            pltpu.VMEM((2, NC, S, CW), BF16),
            pltpu.VMEM((2, NC, S, CW), F32),
            pltpu.VMEM((NC, S, CW), BF16),
            pltpu.VMEM((NC, S, CW), BF16),
            pltpu.VMEM((2 * NC, S, 128), BF16),
            pltpu.VMEM((NC, 8, YR, 128), BF16),
            pltpu.VMEM((NC, YR, 128), F32),
            pltpu.VMEM((NC, 8, WR, 128), F32),
            pltpu.VMEM((2 * NC, WR, 128), F32),
            pltpu.VMEM((T, 2 * Q), BF16),
            pltpu.VMEM((T, D), BF16),
            pltpu.VMEM((OWN, HV), F32),
            pltpu.VMEM((PZ, HV // 2), F32),
            pltpu.VMEM((2, 2, PZ, HV // 2), BF16),
            pltpu.VMEM((YR, HV // 2), F32),
            pltpu.VMEM((2, S, HV // 2), BF16),
            dma((6 + NT,)), dma((6 + NT,)),
            dma((5 + 2 * NC,)), dma((5 + 2 * NC,)),
            dma((NZ + NC,)), dma((NZ + NC,)),
            dma((2,)), dma((2,)),
            dma((3 + 7 * NC,)), dma((3 + 7 * NC,)),
            dma((17,)), dma((17,)),
            dma((10,)),
        ],
        compiler_params=pltpu.CompilerParams(
            collective_id=0, has_side_effects=True, vmem_limit_bytes=54 * 1024 * 1024
        ),
        cost_estimate=pl.CostEstimate(
            flops=4 * T * D * HV, bytes_accessed=16 * 1024 * 1024, transcendentals=T
        ),
        name="diloco",
    )(params[0], tokens[0], cotangent[0], gain, glob, momentum, prev_global)
    out = pl.pallas_call(
        store,
        out_shape=tuple(jax.ShapeDtypeStruct(v.shape, v.dtype) for v in out),
        in_specs=[vmem] * len(out),
        out_specs=[hbm] * len(out),
        scratch_shapes=[dma((9,))],
        compiler_params=pltpu.CompilerParams(vmem_limit_bytes=1024 * 1024),
        name="store",
    )(*out)
    return (out[0][None], out[1][None], out[2], out[3])


def solution(mesh):
    placed = (
        P("replica", "fsdp", None),
        P("replica", "fsdp", None),
        P("replica", "fsdp", None),
        P(),
        P(("fsdp", "replica"), None),
        P(("fsdp", "replica"), None),
        P(("fsdp", "replica"), None),
    )
    return jax.shard_map(
        shards,
        mesh=mesh,
        in_specs=placed,
        out_specs=(
            P("replica", "fsdp", None),
            P("replica", "fsdp", None),
            P(("fsdp", "replica"), None),
            P(("fsdp", "replica"), None),
        ),
        check_vma=False,
    )
```

```python
import jax
import jax.numpy as jnp
from jax import lax
from jax.experimental import pallas as pl
from jax.experimental.pallas import tpu as pltpu
from jax.sharding import PartitionSpec as P

inner_rate = 0.5
outer_rate = 0.7
nesterov = 0.9
mix_weight = 0.5
eps = 1e-06

MESH = pl.DeviceIdType.MESH
F32 = jnp.float32
BF16 = jnp.bfloat16

D = 4608
HV = 1024
T = 512
Q = 1152
S = 576
NC = 4
CW = HV // NC
NT = 8
TR = T // NT
NZ = 4
ZR = S // NZ
YR = S // 4
WR = 24
OWN = 18
PZ = 48


def pieces(core):
    out = []
    for plane in (0, D // 2):
        out.append((plane, pl.multiple_of(plane + core * Q, 128), 512))
        out.append((plane + 512, pl.multiple_of(plane + (1 - core) * 512, 128), Q))
        out.append((plane + 512 + Q, plane + 512 + Q, Q - 512))
    return out


def kernel(
    params, tokens, cot, gain, glob, mom, prev,
    new_params, tok, new_global, new_momentum,
    cc, invb, gn, gv, nst, nnt, wg, gs, gr, gk, zs, zr, up, yr, s8, lr, tot,
    xs, xa, po, pz, pzr, pa, pfull,
    a_s, a_r, b_s, b_r, z_s, z_r, c_s, c_r, y_s, y_r, l_s, l_r, loc,
):
    rep = lax.axis_index("replica")
    fs = lax.axis_index("fsdp")
    core = lax.rem(rep, 2)
    zl = lax.rem(lax.div(rep, 2), 4)
    y = lax.div(rep, 8)
    x = lax.rem(fs, 4)
    zh = lax.div(fs, 4)
    half = jnp.where(core == 0, lax.div(x, 2), 1 - lax.rem(lax.div(x + 1, 2), 2))
    par = jnp.where(core == 0, lax.rem(x, 2), lax.div(x, 2))
    beside = x + 1 - 2 * lax.rem(x, 2)

    dev_a = (rep, zh * 4 + jnp.where(core == 0, 3 - x, beside))
    dev_b = (rep, zh * 4 + jnp.where(core == 0, beside, 3 - x))
    dev_z = (rep, (1 - zh) * 4 + x)
    dev_c = ((y * 4 + zl) * 2 + (1 - core), fs)

    def dev_y(i):
        return ((lax.rem(y + i // 2, 4) * 4 + zl) * 2 + lax.rem(core + i % 2, 2), fs)

    def dev_l(i):
        return ((y * 4 + lax.rem(zl + i // 2, 4)) * 2 + lax.rem(core + i % 2, 2), fs)

    def dev_zl(pos):
        return ((y * 4 + pos) * 2 + core, fs)

    def remote(src, dst, sends, recvs, i, dev):
        return pltpu.make_async_remote_copy(
            src_ref=src,
            dst_ref=dst,
            send_sem=sends.at[i],
            recv_sem=recvs.at[i],
            device_id=dev,
            device_id_type=MESH,
        )

    def column(b):
        plane = (1 - zh) if b % 2 == 0 else zh
        side = (1 - half) if b < 2 else half
        return pl.multiple_of(plane * (D // 2) + side * Q, 128)

    def tile(b, j):
        return pl.ds(pl.multiple_of(column(b) + j * 128, 128), 128)

    my_rows = pl.multiple_of(par * S, 64)
    its_rows = pl.multiple_of((1 - par) * S, 64)
    base = jnp.where((core == 1) & (half == 0), 64, 0)
    w_rows = pl.multiple_of(base + par * S, 64)

    def w_part(k):
        return pl.ds(pl.multiple_of(w_rows + k * ZR, 16), ZR)

    first_lanes = (lax.broadcasted_iota(jnp.int32, (16, 128), 1) < 64) & (core == 1)

    def exchange(v, u, mask):
        return jnp.where(mask, u, v), jnp.where(mask, v, u)

    loads = [
        pltpu.make_async_copy(
            tokens.at[:, pl.ds(start, width)], tok.at[:, pl.ds(place, width)], loc.at[4 + i]
        )
        for i, (start, place, width) in enumerate(pieces(core))
    ]
    loads.append(pltpu.make_async_copy(gain, gn.at[0], loc.at[1]))
    load_cot = pltpu.make_async_copy(cot, cc.at[pl.ds(0, T)], loc.at[2])
    load_w = pltpu.make_async_copy(params, wg.at[1, pl.ds(w_rows, S)], loc.at[3])

    barrier = pltpu.get_barrier_semaphore()
    peers = [dev_a, dev_b, dev_z] + [dev_y(i) for i in range(1, 8)] + [dev_l(i) for i in range(2, 8)]
    for dev in peers:
        pl.semaphore_signal(barrier, inc=1, device_id=dev, device_id_type=MESH)
    for cp in loads:
        cp.start()
    load_cot.start()
    load_w.start()
    pl.semaphore_wait(barrier, len(peers))

    send_prev = remote(prev, po, c_s, c_r, 0, dev_c)
    send_prev.start()
    send_cot = remote(cot, cc.at[pl.ds(T, T)], a_s, a_r, 0, dev_a)
    send_cot.start()
    send_w = remote(params, wg.at[1, pl.ds(w_rows, S)], b_s, b_r, 0, dev_b)
    send_w.start()
    far_w = [
        remote(
            params.at[pl.ds(k * ZR, ZR)],
            wg.at[0, w_part(k)],
            z_s, z_r, k, dev_z,
        )
        for k in range(NZ)
    ]
    far_w[0].start()

    send_prev.wait_recv()
    wide = pl.ds(pl.multiple_of(core * (HV // 2), 128), HV // 2)
    pz[...] = jnp.zeros_like(pz)

    @pl.when(core == 0)
    def _():
        pz[0:OWN, :] = prev[:, wide]
        pz[OWN : 2 * OWN, :] = po[:, wide]

    @pl.when(core == 1)
    def _():
        pz[0:OWN, :] = po[:, wide]
        pz[OWN : 2 * OWN, :] = prev[:, wide]

    pair, place_in = lax.div(zl, 2), lax.rem(zl, 2)
    edge = pair == place_in
    pzr[pair, place_in] = pz[...].astype(BF16)
    prev_l = remote(
        pzr.at[pair, place_in], pzr.at[pair, place_in], l_s, l_r, 0, dev_zl(zl + 1 - 2 * place_in)
    )
    prev_l.start()
    for cp in far_w[1:]:
        cp.start()

    relay = [
        pltpu.make_async_remote_copy(
            src_ref=pzr.at[pair],
            dst_ref=pzr.at[pair],
            send_sem=l_s.at[1 + k],
            recv_sem=l_r.at[1],
            device_id=dev_zl((1 - pair) * 2 + k),
            device_id_type=MESH,
        )
        for k in range(2)
    ]

    def pass_prev():
        prev_l.wait_recv()

        @pl.when(edge)
        def _():
            for cp in relay:
                cp.start()

    for cp in loads:
        cp.wait()
    for start, place, width in pieces(core):
        gv[:, pl.ds(place, width)] = gn[:, start : start + width]
    for plane in (0, D // 2):
        at, to = slice(plane, plane + 128), slice(plane + 512 + Q, plane + 640 + Q)
        gv[:, at], gv[:, to] = exchange(gv[:, at], gv[:, to], first_lanes[0:1, :])

        @pl.when(core == 1)
        def _():
            @pl.loop(0, T // 16)
            def _(i):
                rows = pl.ds(pl.multiple_of(i * 16, 16), 16)
                v, u = exchange(tok[rows, at].astype(F32), tok[rows, to].astype(F32), first_lanes)
                tok[rows, at] = v.astype(BF16)
                tok[rows, to] = u.astype(BF16)


    @pl.loop(0, T // 32)
    def _(i):
        rows = pl.ds(pl.multiple_of(i * 32, 32), 32)
        acc = jnp.zeros((32, 128), F32)
        for j in range(D // 128):
            v = tok[rows, j * 128 : (j + 1) * 128].astype(F32)
            acc = acc + v * v
        inv = lax.rsqrt(jnp.sum(acc, axis=-1, keepdims=True) * (1.0 / D) + eps)
        invb[rows, :] = jnp.broadcast_to(inv, (32, 128))

    def normed(b, put):
        @pl.loop(0, Q // 128)
        def _(j):
            cols = tile(b, j)
            v = (tok[:, cols].astype(F32) * invb[...] * gv[:, cols]).T.astype(BF16)
            side = (1 - half) if b < 2 else half
            shift = jnp.where((core == 1) & (side == 0), 64, 0)
            for k in range(2):
                row = lax.rem(j * 128 + k * 64 - shift + Q, Q)
                put(pl.ds(pl.multiple_of(row, 64), 64), v[k * 64 : (k + 1) * 64])

    def put_send(o):
        def put(rows, v):
            nst[o, rows, :] = v
        return put

    def put_own(o):
        def put(rows, v):
            nnt[o, rows, 0:T] = v
        return put

    send_n = []
    for o in range(2):
        normed(o, put_send(o))
        for p in range(2):
            rows = pl.ds(pl.multiple_of(jnp.where(core == p, my_rows, its_rows), 64), S)
            cp = remote(nst.at[o, rows], nnt.at[o, rows, pl.ds(T, T)], a_s, a_r, 1 + 2 * o + p, dev_a)
            cp.start()
            send_n.append(cp)

    for o in range(2):
        normed(2 + o, put_own(o))

    y_rows = pl.ds(pl.multiple_of(y * YR, 16), YR)
    prev_y = []

    def prev_to_y():
        relay[0].wait_recv()
        for k in range(4):
            pa[k * 36 : (k + 1) * 36, :] = pzr[k // 2, k % 2, 0:36, :].astype(F32)
        pfull[core, y_rows, :] = pa[...].astype(BF16)
        prev_y.extend(
            [
                remote(pfull.at[core, y_rows], pfull.at[core, y_rows], y_s, y_r, d, dev_y(2 * d + 2))
                for d in range(3)
            ]
        )
        for cp in prev_y:
            cp.start()

    forward = [
        remote(
            wg.at[0, w_part(k)],
            wg.at[0, w_part(k)],
            b_s, b_r, 1 + k, dev_b,
        )
        for k in range(NZ)
    ]

    def pass_on(k):
        far_w[k].wait_recv()
        forward[k].start()

    def send_g(o, c):
        return remote(gs.at[o, c], gr.at[o, c], b_s, b_r, 5 + NC * o + c, dev_b)

    def product(o, rows, c):
        cols = pl.ds(pl.multiple_of(c * CW, 128), CW)
        return jnp.dot(nnt[o, pl.ds(rows, S), :], cc[:, cols], preferred_element_type=F32)

    def give(o):
        send_n[2 * o].wait_recv()

        @pl.loop(0, NC)
        def _(c):
            gs[o, c] = product(o, its_rows, c).astype(BF16)
            send_g(o, c).start()

    def keep(o):
        send_n[2 * o + 1].wait_recv()

        @pl.loop(0, NC)
        def _(c):
            gk[o, c] = product(o, my_rows, c)

    def send_s(c):
        return remote(zs.at[c], zr.at[c], z_s, z_r, NZ + c, dev_z)

    def far_sum(c):
        send_g(0, c).wait_recv()
        zs[c] = (gk[0, c] + gr[0, c].astype(F32)).astype(BF16)
        send_s(c).start()

    def wrap(o):
        @pl.when(base == 64)
        def _():
            wg[o, 0:64, :] = wg[o, Q : Q + 64, :]

    def dn(o, first, put):
        @pl.loop(0, 3)
        def _(n):
            rows = pl.ds(pl.multiple_of(n * 384, 128), 384)
            put(
                o,
                n * 384,
                lax.dot_general(
                    cc[first : first + T, :],
                    wg[o, rows, :],
                    (((1,), (1,)), ((), ())),
                    preferred_element_type=F32,
                ),
            )

    def own_columns(o, at):
        return pl.ds(pl.multiple_of(column(2 + o) + at, 128), 384)

    def put_xs(o, at, v):
        scaled = v * gv[:, own_columns(o, at)]
        xs[:, pl.ds(pl.multiple_of(o * Q + at, 128), 384)] = scaled.astype(BF16)

    def put_xo(o, at, v):
        scaled = v * gv[:, own_columns(o, at)]
        xa[:, own_columns(o, at)] = scaled.astype(BF16)

    own_plane = pl.ds(Q, Q)
    send_x1 = remote(
        xs.at[:, own_plane], xa.at[:, pl.ds(column(3), Q)], a_s, a_r, 5 + NT, dev_a
    )
    send_x = []
    for t in range(NT):
        rows = pl.ds(t * TR, TR)
        send_x.append(
            remote(xs.at[rows, pl.ds(0, Q)], xa.at[rows, pl.ds(column(2), Q)], a_s, a_r, 5 + t, dev_a)
        )

    def finish(t):
        send_x[t].wait_recv()

        @pl.loop(0, TR // 16)
        def _(i):
            rows = pl.ds(pl.multiple_of(t * TR + i * 16, 16), 16)
            inv = invb[rows, :]

            def parts(j):
                cols = slice(j * 128, (j + 1) * 128)
                return tok[rows, cols].astype(F32), xa[rows, cols].astype(F32)

            acc = jnp.zeros((16, 128), F32)
            for j in range(D // 128):
                v, scaled = parts(j)
                acc = acc + v * scaled
            weight = inv * inv * inv * (jnp.sum(acc, axis=-1, keepdims=True) * (1.0 / D))

            def result(j):
                v, scaled = parts(j)
                return inv * scaled - weight * v

            def put(j, v):
                tok[rows, j * 128 : (j + 1) * 128] = v.astype(BF16)

            for plane in (0, D // 256):
                last = plane + (512 + Q) // 128
                v, u = exchange(result(plane), result(last), first_lanes)
                put(plane, v)
                put(last, u)
                for j in range(plane + 1, plane + D // 256):
                    if j != last:
                        put(j, result(j))

    def send_y(c, i):
        rows = pl.ds(pl.multiple_of(lax.rem(y + i // 2, 4) * YR, 16), YR)
        src = up.at[2 * c + lax.rem(core + i % 2, 2), rows]
        return remote(src, yr.at[c, i], y_s, y_r, 3 + c, dev_y(i))

    def window(pos):
        return pl.ds(pl.multiple_of(lax.div(pos * OWN, 8) * 8, 8), WR)

    def send_l(first, count, i):
        pos = lax.rem(zl + i // 2, 4) * 2 + lax.rem(core + i % 2, 2)
        chunks = pl.ds(first, count)
        sem = 4 if first else 3
        return remote(s8.at[chunks, window(pos)], lr.at[chunks, i], l_s, l_r, sem, dev_l(i))

    def all_of(ref, sem):
        pltpu.make_async_copy(ref, ref, sem).wait()

    def seven_y(c, sems):
        all_of(yr.at[c, pl.ds(1, 7)], sems.at[3 + c])

    def seven_l(first, count, sems):
        all_of(lr.at[pl.ds(first, count), pl.ds(1, 7)], sems.at[4 if first else 3])

    def update(c):
        send_g(1, c).wait_recv()
        send_s(c).wait_recv()
        for k in range(2):
            part = slice(k * 128, (k + 1) * 128)
            cols = slice(c * CW + k * 128, c * CW + (k + 1) * 128)
            grad = gk[1, c, :, part] + gr[1, c, :, part].astype(F32) + zr[c, :, part].astype(F32)
            now = (wg[1, pl.ds(w_rows, S), cols].astype(F32) - inner_rate * grad).astype(BF16)
            up[2 * c + k] = now
        for i in (4, 5, 2, 3, 6, 7, 1):
            send_y(c, i).start()

    def mix(c):
        for k in range(2):
            cols = slice(c * CW + k * 128, c * CW + (k + 1) * 128)
            at = (c % 2) * CW + k * 128
            old = pfull[c // 2, :, at : at + 128].astype(F32)
            new_params[:, cols] = (
                (1.0 - mix_weight) * up[2 * c + k].astype(F32) + mix_weight * old
            ).astype(BF16)

    def all_y(c):
        seven_y(c, y_r)
        total = up[2 * c + core, y_rows, :].astype(F32)
        for i in range(1, 8):
            total = total + yr[c, i].astype(F32)
        s8[c] = total

    far_first = (4, 5, 2, 3, 6, 7, 1)

    def start_l(first, count):
        for i in far_first:
            send_l(first, count, i).start()

    def all_l(first, count):
        seven_l(first, count, l_r)
        for c in range(first, first + count):
            tot[2 * c + core] = s8[c, window(zl * 2 + core), :] + lr[c, 2] + lr[c, 4] + lr[c, 6]
            tot[2 * c + 1 - core] = lr[c, 1] + lr[c, 3] + lr[c, 5] + lr[c, 7]

    def sent(*copies):
        for cp in copies:
            cp.wait_send()

    pass_on(0)
    pass_on(1)
    pass_prev()
    load_cot.wait()
    load_w.wait()
    send_cot.wait_recv()
    give(0)
    send_w.wait_recv()
    wrap(1)
    dn(1, T, put_xs)
    send_x1.start()
    pass_on(2)
    keep(0)
    far_sum(0)
    far_sum(1)
    pass_on(3)
    far_sum(2)
    give(1)
    far_sum(3)
    dn(1, 0, put_xo)
    sent(send_cot, send_w, send_prev, prev_l, *far_w, *send_n[:3])
    keep(1)
    for cp in forward:
        cp.wait_recv()
    wrap(0)
    dn(0, T, put_xs)
    for cp in send_x:
        cp.start()
    dn(0, 0, put_xo)
    sent(send_n[3], *forward, *[send_g(0, c) for c in range(NC)])

    @pl.when(edge)
    def _():
        sent(*relay)

    update(0)
    prev_to_y()
    update(1)
    for cp in prev_y:
        cp.wait_recv()
    prev_c = remote(pfull.at[core], pfull.at[core], c_s, c_r, 1, dev_c)
    prev_c.start()
    all_y(0)
    update(2)
    prev_c.wait_recv()
    mix(0)
    mix(1)
    all_y(1)
    send_x1.wait_recv()
    finish(0)
    mix(2)
    finish(1)
    finish(2)
    sent(prev_c, send_x1, *prev_y, *[send_g(1, c) for c in range(NC)])
    update(3)
    all_y(2)
    start_l(0, 3)
    finish(3)
    finish(4)
    finish(5)
    all_y(3)
    start_l(3, 1)
    mix(3)
    finish(6)
    finish(7)
    sent(*send_x, *[send_s(c) for c in range(NC)])
    for c in range(NC):
        seven_y(c, y_s)
    all_l(0, 3)
    all_l(3, 1)

    place = lax.rem(zl, 2) * 2 + core
    for j in range(HV // 128):
        cols = slice(j * 128, (j + 1) * 128)
        total = jnp.where(
            place < 2,
            jnp.where(place == 0, tot[j, 0:18, :], tot[j, 2:20, :]),
            jnp.where(place == 2, tot[j, 4:22, :], tot[j, 6:24, :]),
        )
        delta = glob[:, cols] - total * (1.0 / 32)
        moved = nesterov * mom[:, cols] + delta
        new_momentum[:, cols] = moved
        new_global[:, cols] = glob[:, cols] - outer_rate * (delta + nesterov * moved)

    seven_l(0, 3, l_s)
    seven_l(3, 1, l_s)


def store(params, tok, glob, mom, params_out, tokens_out, glob_out, mom_out, sems):
    core = lax.rem(lax.axis_index("replica"), 2)
    copies = [
        pltpu.make_async_copy(
            tok.at[:, pl.ds(place, width)], tokens_out.at[:, pl.ds(start, width)], sems.at[i]
        )
        for i, (start, place, width) in enumerate(pieces(core))
    ]
    n = len(copies)
    for i, (src, dst) in enumerate(((params, params_out), (glob, glob_out), (mom, mom_out))):
        copies.append(pltpu.make_async_copy(src, dst, sems.at[n + i]))
    for cp in copies:
        cp.start()
    for cp in copies:
        cp.wait()


def shards(params, tokens, cotangent, gain, glob, momentum, prev_global):
    vmem = pl.BlockSpec(memory_space=pltpu.VMEM)
    hbm = pl.BlockSpec(memory_space=pl.ANY)
    dma = pltpu.SemaphoreType.DMA
    out = pl.pallas_call(
        kernel,
        out_shape=(
            pltpu.VMEM((S, HV), BF16),
            pltpu.VMEM((T, D), BF16),
            pltpu.VMEM((OWN, HV), F32),
            pltpu.VMEM((OWN, HV), F32),
        ),
        in_specs=[hbm, hbm, hbm, hbm, vmem, vmem, vmem],
        out_specs=(vmem, vmem, vmem, vmem),
        scratch_shapes=[
            pltpu.VMEM((2 * T, HV), BF16),
            pltpu.VMEM((T, 128), F32),
            pltpu.VMEM((1, D), F32),
            pltpu.VMEM((1, D), F32),
            pltpu.VMEM((2, Q, T), BF16),
            pltpu.VMEM((2, Q, 2 * T), BF16),
            pltpu.VMEM((2, Q + 64, HV), BF16),
            pltpu.VMEM((2, NC, S, CW), BF16),
            pltpu.VMEM((2, NC, S, CW), BF16),
            pltpu.VMEM((2, NC, S, CW), F32),
            pltpu.VMEM((NC, S, CW), BF16),
            pltpu.VMEM((NC, S, CW), BF16),
            pltpu.VMEM((2 * NC, S, 128), BF16),
            pltpu.VMEM((NC, 8, YR, 128), BF16),
            pltpu.VMEM((NC, YR, 128), F32),
            pltpu.VMEM((NC, 8, WR, 128), F32),
            pltpu.VMEM((2 * NC, WR, 128), F32),
            pltpu.VMEM((T, 2 * Q), BF16),
            pltpu.VMEM((T, D), BF16),
            pltpu.VMEM((OWN, HV), F32),
            pltpu.VMEM((PZ, HV // 2), F32),
            pltpu.VMEM((2, 2, PZ, HV // 2), BF16),
            pltpu.VMEM((YR, HV // 2), F32),
            pltpu.VMEM((2, S, HV // 2), BF16),
            dma((6 + NT,)), dma((6 + NT,)),
            dma((5 + 2 * NC,)), dma((5 + 2 * NC,)),
            dma((NZ + NC,)), dma((NZ + NC,)),
            dma((2,)), dma((2,)),
            dma((3 + NC,)), dma((3 + NC,)),
            dma((5,)), dma((5,)),
            dma((10,)),
        ],
        compiler_params=pltpu.CompilerParams(
            collective_id=0, has_side_effects=True, vmem_limit_bytes=54 * 1024 * 1024
        ),
        cost_estimate=pl.CostEstimate(
            flops=4 * T * D * HV, bytes_accessed=16 * 1024 * 1024, transcendentals=T
        ),
        name="diloco",
    )(params[0], tokens[0], cotangent[0], gain, glob, momentum, prev_global)
    out = pl.pallas_call(
        store,
        out_shape=tuple(jax.ShapeDtypeStruct(v.shape, v.dtype) for v in out),
        in_specs=[vmem] * len(out),
        out_specs=[hbm] * len(out),
        scratch_shapes=[dma((9,))],
        compiler_params=pltpu.CompilerParams(vmem_limit_bytes=1024 * 1024),
        name="store",
    )(*out)
    return (out[0][None], out[1][None], out[2], out[3])


def solution(mesh):
    placed = (
        P("replica", "fsdp", None),
        P("replica", "fsdp", None),
        P("replica", "fsdp", None),
        P(),
        P(("fsdp", "replica"), None),
        P(("fsdp", "replica"), None),
        P(("fsdp", "replica"), None),
    )
    return jax.shard_map(
        shards,
        mesh=mesh,
        in_specs=placed,
        out_specs=(
            P("replica", "fsdp", None),
            P("replica", "fsdp", None),
            P(("fsdp", "replica"), None),
            P(("fsdp", "replica"), None),
        ),
        check_vma=False,
    )
```

```python
import jax
import jax.numpy as jnp
from jax import lax
from jax.experimental import pallas as pl
from jax.experimental.pallas import tpu as pltpu
from jax.sharding import PartitionSpec as P

inner_rate = 0.5
outer_rate = 0.7
nesterov = 0.9
mix_weight = 0.5
eps = 1e-06

MESH = pl.DeviceIdType.MESH
F32 = jnp.float32
BF16 = jnp.bfloat16

D = 4608
HV = 1024
T = 512
Q = 1152
S = 576
NC = 4
CW = HV // NC
NT = 8
TR = T // NT
NZ = 4
ZR = S // NZ
YR = S // 4
WR = 24
OWN = 18
PZ = 48


def pieces(core):
    out = []
    for plane in (0, D // 2):
        out.append((plane, pl.multiple_of(plane + core * Q, 128), 512))
        out.append((plane + 512, pl.multiple_of(plane + (1 - core) * 512, 128), Q))
        out.append((plane + 512 + Q, plane + 512 + Q, Q - 512))
    return out


def kernel(
    params, tokens, cot, gain, glob, mom, prev,
    new_params, tok, new_global, new_momentum,
    cc, invb, gn, gv, nst, nnt, wg, gs, gr, gk, zs, zr, up, yr, s8, lr, tot,
    xs, xa, po, pz, pzr, pa, pfull,
    a_s, a_r, b_s, b_r, z_s, z_r, c_s, c_r, y_s, y_r, l_s, l_r, loc,
):
    rep = lax.axis_index("replica")
    fs = lax.axis_index("fsdp")
    core = lax.rem(rep, 2)
    zl = lax.rem(lax.div(rep, 2), 4)
    y = lax.div(rep, 8)
    x = lax.rem(fs, 4)
    zh = lax.div(fs, 4)
    half = jnp.where(core == 0, lax.div(x, 2), 1 - lax.rem(lax.div(x + 1, 2), 2))
    par = jnp.where(core == 0, lax.rem(x, 2), lax.div(x, 2))
    beside = x + 1 - 2 * lax.rem(x, 2)

    dev_a = (rep, zh * 4 + jnp.where(core == 0, 3 - x, beside))
    dev_b = (rep, zh * 4 + jnp.where(core == 0, beside, 3 - x))
    dev_z = (rep, (1 - zh) * 4 + x)
    dev_c = ((y * 4 + zl) * 2 + (1 - core), fs)

    def dev_y(i):
        return ((lax.rem(y + i // 2, 4) * 4 + zl) * 2 + lax.rem(core + i % 2, 2), fs)

    def dev_l(i):
        return ((y * 4 + lax.rem(zl + i // 2, 4)) * 2 + lax.rem(core + i % 2, 2), fs)

    def dev_zl(pos):
        return ((y * 4 + pos) * 2 + core, fs)

    def remote(src, dst, sends, recvs, i, dev):
        return pltpu.make_async_remote_copy(
            src_ref=src,
            dst_ref=dst,
            send_sem=sends.at[i],
            recv_sem=recvs.at[i],
            device_id=dev,
            device_id_type=MESH,
        )

    def column(b):
        plane = (1 - zh) if b % 2 == 0 else zh
        side = (1 - half) if b < 2 else half
        return pl.multiple_of(plane * (D // 2) + side * Q, 128)

    def tile(b, j):
        return pl.ds(pl.multiple_of(column(b) + j * 128, 128), 128)

    my_rows = pl.multiple_of(par * S, 64)
    its_rows = pl.multiple_of((1 - par) * S, 64)
    base = jnp.where((core == 1) & (half == 0), 64, 0)
    w_rows = pl.multiple_of(base + par * S, 64)

    def w_part(k):
        return pl.ds(pl.multiple_of(w_rows + k * ZR, 16), ZR)

    first_lanes = (lax.broadcasted_iota(jnp.int32, (16, 128), 1) < 64) & (core == 1)

    def exchange(v, u, mask):
        return jnp.where(mask, u, v), jnp.where(mask, v, u)

    loads = [
        pltpu.make_async_copy(
            tokens.at[:, pl.ds(start, width)], tok.at[:, pl.ds(place, width)], loc.at[4 + i]
        )
        for i, (start, place, width) in enumerate(pieces(core))
    ]
    loads.append(pltpu.make_async_copy(gain, gn.at[0], loc.at[1]))
    load_cot = pltpu.make_async_copy(cot, cc.at[pl.ds(0, T)], loc.at[2])
    load_w = pltpu.make_async_copy(params, wg.at[1, pl.ds(w_rows, S)], loc.at[3])

    barrier = pltpu.get_barrier_semaphore()
    peers = [dev_a, dev_b, dev_z] + [dev_y(i) for i in range(1, 8)] + [dev_l(i) for i in range(2, 8)]
    for dev in peers:
        pl.semaphore_signal(barrier, inc=1, device_id=dev, device_id_type=MESH)
    for cp in loads:
        cp.start()
    load_cot.start()
    load_w.start()
    pl.semaphore_wait(barrier, len(peers))

    send_prev = remote(prev, po, c_s, c_r, 0, dev_c)
    send_prev.start()
    send_cot = remote(cot, cc.at[pl.ds(T, T)], a_s, a_r, 0, dev_a)
    send_cot.start()
    send_w = remote(params, wg.at[1, pl.ds(w_rows, S)], b_s, b_r, 0, dev_b)
    send_w.start()
    far_w = [
        remote(
            params.at[pl.ds(k * ZR, ZR)],
            wg.at[0, w_part(k)],
            z_s, z_r, k, dev_z,
        )
        for k in range(NZ)
    ]
    far_w[0].start()

    send_prev.wait_recv()
    wide = pl.ds(pl.multiple_of(core * (HV // 2), 128), HV // 2)
    pz[...] = jnp.zeros_like(pz)

    @pl.when(core == 0)
    def _():
        pz[0:OWN, :] = prev[:, wide]
        pz[OWN : 2 * OWN, :] = po[:, wide]

    @pl.when(core == 1)
    def _():
        pz[0:OWN, :] = po[:, wide]
        pz[OWN : 2 * OWN, :] = prev[:, wide]

    pair, place_in = lax.div(zl, 2), lax.rem(zl, 2)
    edge = pair == place_in
    pzr[pair, place_in] = pz[...].astype(BF16)
    prev_l = remote(
        pzr.at[pair, place_in], pzr.at[pair, place_in], l_s, l_r, 0, dev_zl(zl + 1 - 2 * place_in)
    )
    prev_l.start()
    for cp in far_w[1:]:
        cp.start()

    relay = [
        pltpu.make_async_remote_copy(
            src_ref=pzr.at[pair],
            dst_ref=pzr.at[pair],
            send_sem=l_s.at[1 + k],
            recv_sem=l_r.at[1],
            device_id=dev_zl((1 - pair) * 2 + k),
            device_id_type=MESH,
        )
        for k in range(2)
    ]

    def pass_prev():
        prev_l.wait_recv()

        @pl.when(edge)
        def _():
            for cp in relay:
                cp.start()

    for cp in loads:
        cp.wait()
    for start, place, width in pieces(core):
        gv[:, pl.ds(place, width)] = gn[:, start : start + width]
    for plane in (0, D // 2):
        at, to = slice(plane, plane + 128), slice(plane + 512 + Q, plane + 640 + Q)
        gv[:, at], gv[:, to] = exchange(gv[:, at], gv[:, to], first_lanes[0:1, :])

        @pl.when(core == 1)
        def _():
            @pl.loop(0, T // 16)
            def _(i):
                rows = pl.ds(pl.multiple_of(i * 16, 16), 16)
                v, u = exchange(tok[rows, at].astype(F32), tok[rows, to].astype(F32), first_lanes)
                tok[rows, at] = v.astype(BF16)
                tok[rows, to] = u.astype(BF16)


    @pl.loop(0, T // 32)
    def _(i):
        rows = pl.ds(pl.multiple_of(i * 32, 32), 32)
        acc = jnp.zeros((32, 128), F32)
        for j in range(D // 128):
            v = tok[rows, j * 128 : (j + 1) * 128].astype(F32)
            acc = acc + v * v
        inv = lax.rsqrt(jnp.sum(acc, axis=-1, keepdims=True) * (1.0 / D) + eps)
        invb[rows, :] = jnp.broadcast_to(inv, (32, 128))

    def normed(b, put):
        @pl.loop(0, Q // 128)
        def _(j):
            cols = tile(b, j)
            v = (tok[:, cols].astype(F32) * invb[...] * gv[:, cols]).T.astype(BF16)
            side = (1 - half) if b < 2 else half
            shift = jnp.where((core == 1) & (side == 0), 64, 0)
            for k in range(2):
                row = lax.rem(j * 128 + k * 64 - shift + Q, Q)
                put(pl.ds(pl.multiple_of(row, 64), 64), v[k * 64 : (k + 1) * 64])

    def put_send(o):
        def put(rows, v):
            nst[o, rows, :] = v
        return put

    def put_own(o):
        def put(rows, v):
            nnt[o, rows, 0:T] = v
        return put

    send_n = []
    for o in range(2):
        normed(o, put_send(o))
        for p in range(2):
            rows = pl.ds(pl.multiple_of(jnp.where(core == p, my_rows, its_rows), 64), S)
            cp = remote(nst.at[o, rows], nnt.at[o, rows, pl.ds(T, T)], a_s, a_r, 1 + 2 * o + p, dev_a)
            cp.start()
            send_n.append(cp)

    for o in range(2):
        normed(2 + o, put_own(o))

    y_rows = pl.ds(pl.multiple_of(y * YR, 16), YR)
    prev_y = []

    def prev_to_y():
        relay[0].wait_recv()
        for k in range(4):
            pa[k * 36 : (k + 1) * 36, :] = pzr[k // 2, k % 2, 0:36, :].astype(F32)
        pfull[core, y_rows, :] = pa[...].astype(BF16)
        prev_y.extend(
            [
                remote(pfull.at[core, y_rows], pfull.at[core, y_rows], y_s, y_r, d, dev_y(2 * d + 2))
                for d in range(3)
            ]
        )
        for cp in prev_y:
            cp.start()

    forward = [
        remote(
            wg.at[0, w_part(k)],
            wg.at[0, w_part(k)],
            b_s, b_r, 1 + k, dev_b,
        )
        for k in range(NZ)
    ]

    def pass_on(k):
        far_w[k].wait_recv()
        forward[k].start()

    def send_g(o, c):
        return remote(gs.at[o, c], gr.at[o, c], b_s, b_r, 5 + NC * o + c, dev_b)

    def product(o, rows, c):
        cols = pl.ds(pl.multiple_of(c * CW, 128), CW)
        return jnp.dot(nnt[o, pl.ds(rows, S), :], cc[:, cols], preferred_element_type=F32)

    def give(o):
        send_n[2 * o].wait_recv()

        @pl.loop(0, NC)
        def _(c):
            gs[o, c] = product(o, its_rows, c).astype(BF16)
            send_g(o, c).start()

    def keep(o):
        send_n[2 * o + 1].wait_recv()

        @pl.loop(0, NC)
        def _(c):
            gk[o, c] = product(o, my_rows, c)

    def send_s(c, h):
        rows = pl.ds(h * (S // 2), S // 2) if c == NC - 1 else pl.ds(0, S)
        return remote(zs.at[c, rows], zr.at[c, rows], z_s, z_r, NZ + c + h, dev_z)

    def far_sum(c):
        send_g(0, c).wait_recv()
        zs[c] = (gk[0, c] + gr[0, c].astype(F32)).astype(BF16)
        for h in range(2 if c == NC - 1 else 1):
            send_s(c, h).start()

    def wrap(o):
        @pl.when(base == 64)
        def _():
            wg[o, 0:64, :] = wg[o, Q : Q + 64, :]

    def dn(o, first, put):
        @pl.loop(0, 3)
        def _(n):
            rows = pl.ds(pl.multiple_of(n * 384, 128), 384)
            put(
                o,
                n * 384,
                lax.dot_general(
                    cc[first : first + T, :],
                    wg[o, rows, :],
                    (((1,), (1,)), ((), ())),
                    preferred_element_type=F32,
                ),
            )

    def own_columns(o, at):
        return pl.ds(pl.multiple_of(column(2 + o) + at, 128), 384)

    def put_xs(o, at, v):
        scaled = v * gv[:, own_columns(o, at)]
        xs[:, pl.ds(pl.multiple_of(o * Q + at, 128), 384)] = scaled.astype(BF16)

    def put_xo(o, at, v):
        scaled = v * gv[:, own_columns(o, at)]
        xa[:, own_columns(o, at)] = scaled.astype(BF16)

    own_plane = pl.ds(Q, Q)
    send_x1 = remote(
        xs.at[:, own_plane], xa.at[:, pl.ds(column(3), Q)], a_s, a_r, 5 + NT, dev_a
    )
    send_x = []
    for t in range(NT):
        rows = pl.ds(t * TR, TR)
        send_x.append(
            remote(xs.at[rows, pl.ds(0, Q)], xa.at[rows, pl.ds(column(2), Q)], a_s, a_r, 5 + t, dev_a)
        )

    def finish(t):
        send_x[t].wait_recv()

        @pl.loop(0, TR // 16)
        def _(i):
            rows = pl.ds(pl.multiple_of(t * TR + i * 16, 16), 16)
            inv = invb[rows, :]

            def parts(j):
                cols = slice(j * 128, (j + 1) * 128)
                return tok[rows, cols].astype(F32), xa[rows, cols].astype(F32)

            acc = jnp.zeros((16, 128), F32)
            for j in range(D // 128):
                v, scaled = parts(j)
                acc = acc + v * scaled
            weight = inv * inv * inv * (jnp.sum(acc, axis=-1, keepdims=True) * (1.0 / D))

            def result(j):
                v, scaled = parts(j)
                return inv * scaled - weight * v

            def put(j, v):
                tok[rows, j * 128 : (j + 1) * 128] = v.astype(BF16)

            for plane in (0, D // 256):
                last = plane + (512 + Q) // 128
                v, u = exchange(result(plane), result(last), first_lanes)
                put(plane, v)
                put(last, u)
                for j in range(plane + 1, plane + D // 256):
                    if j != last:
                        put(j, result(j))

    def send_y(c, i):
        rows = pl.ds(pl.multiple_of(lax.rem(y + i // 2, 4) * YR, 16), YR)
        src = up.at[2 * c + lax.rem(core + i % 2, 2), rows]
        return remote(src, yr.at[c, i], y_s, y_r, 3 + c, dev_y(i))

    def window(pos):
        return pl.ds(pl.multiple_of(lax.div(pos * OWN, 8) * 8, 8), WR)

    def send_l(first, count, i):
        pos = lax.rem(zl + i // 2, 4) * 2 + lax.rem(core + i % 2, 2)
        chunks = pl.ds(first, count)
        sem = 4 if first else 3
        return remote(s8.at[chunks, window(pos)], lr.at[chunks, i], l_s, l_r, sem, dev_l(i))

    def all_of(ref, sem):
        pltpu.make_async_copy(ref, ref, sem).wait()

    def seven_y(c, sems):
        all_of(yr.at[c, pl.ds(1, 7)], sems.at[3 + c])

    def seven_l(first, count, sems):
        all_of(lr.at[pl.ds(first, count), pl.ds(1, 7)], sems.at[4 if first else 3])

    def update(c):
        send_g(1, c).wait_recv()
        halves = 2 if c == NC - 1 else 1
        for h in range(halves):
            send_s(c, h).wait_recv()
            rows = slice(h * (S // 2), (h + 1) * (S // 2)) if halves == 2 else slice(0, S)
            w_here = pl.ds(pl.multiple_of(w_rows + rows.start, 16), rows.stop - rows.start)
            for k in range(2):
                part = slice(k * 128, (k + 1) * 128)
                cols = slice(c * CW + k * 128, c * CW + (k + 1) * 128)
                grad = gk[1, c, rows, part] + gr[1, c, rows, part].astype(F32) + zr[c, rows, part].astype(F32)
                now = (wg[1, w_here, cols].astype(F32) - inner_rate * grad).astype(BF16)
                up[2 * c + k, rows] = now
            for i in (4, 5, 2, 3, 6, 7, 1):
                if halves == 1:
                    send_y(c, i).start()
                else:

                    @pl.when(lax.div(lax.rem(y + i // 2, 4), 2) == h)
                    def _():
                        send_y(c, i).start()

    def mix(c):
        for k in range(2):
            cols = slice(c * CW + k * 128, c * CW + (k + 1) * 128)
            at = (c % 2) * CW + k * 128
            old = pfull[c // 2, :, at : at + 128].astype(F32)
            new_params[:, cols] = (
                (1.0 - mix_weight) * up[2 * c + k].astype(F32) + mix_weight * old
            ).astype(BF16)

    def all_y(c):
        seven_y(c, y_r)
        total = up[2 * c + core, y_rows, :].astype(F32)
        for i in range(1, 8):
            total = total + yr[c, i].astype(F32)
        s8[c] = total

    far_first = (4, 5, 2, 3, 6, 7, 1)

    def start_l(first, count):
        for i in far_first:
            send_l(first, count, i).start()

    def all_l(first, count):
        seven_l(first, count, l_r)
        for c in range(first, first + count):
            tot[2 * c + core] = s8[c, window(zl * 2 + core), :] + lr[c, 2] + lr[c, 4] + lr[c, 6]
            tot[2 * c + 1 - core] = lr[c, 1] + lr[c, 3] + lr[c, 5] + lr[c, 7]

    def sent(*copies):
        for cp in copies:
            cp.wait_send()

    pass_on(0)
    pass_on(1)
    pass_prev()
    load_cot.wait()
    load_w.wait()
    send_cot.wait_recv()
    give(0)
    send_w.wait_recv()
    wrap(1)
    dn(1, T, put_xs)
    send_x1.start()
    pass_on(2)
    keep(0)
    far_sum(0)
    far_sum(1)
    pass_on(3)
    far_sum(2)
    give(1)
    far_sum(3)
    dn(1, 0, put_xo)
    sent(send_cot, send_w, send_prev, prev_l, *far_w, *send_n[:3])
    keep(1)
    for cp in forward:
        cp.wait_recv()
    wrap(0)
    dn(0, T, put_xs)
    for cp in send_x:
        cp.start()
    dn(0, 0, put_xo)
    sent(send_n[3], *forward, *[send_g(0, c) for c in range(NC)])

    @pl.when(edge)
    def _():
        sent(*relay)

    update(0)
    prev_to_y()
    update(1)
    for cp in prev_y:
        cp.wait_recv()
    prev_c = remote(pfull.at[core], pfull.at[core], c_s, c_r, 1, dev_c)
    prev_c.start()
    all_y(0)
    update(2)
    prev_c.wait_recv()
    mix(0)
    mix(1)
    all_y(1)
    send_x1.wait_recv()
    finish(0)
    mix(2)
    finish(1)
    finish(2)
    sent(prev_c, send_x1, *prev_y, *[send_g(1, c) for c in range(NC)])
    update(3)
    all_y(2)
    start_l(0, 3)
    finish(3)
    finish(4)
    finish(5)
    all_y(3)
    start_l(3, 1)
    mix(3)
    finish(6)
    finish(7)
    sent(*send_x, *[send_s(c, 0) for c in range(NC)], send_s(NC - 1, 1))
    for c in range(NC):
        seven_y(c, y_s)
    all_l(0, 3)
    all_l(3, 1)

    place = lax.rem(zl, 2) * 2 + core
    for j in range(HV // 128):
        cols = slice(j * 128, (j + 1) * 128)
        total = jnp.where(
            place < 2,
            jnp.where(place == 0, tot[j, 0:18, :], tot[j, 2:20, :]),
            jnp.where(place == 2, tot[j, 4:22, :], tot[j, 6:24, :]),
        )
        delta = glob[:, cols] - total * (1.0 / 32)
        moved = nesterov * mom[:, cols] + delta
        new_momentum[:, cols] = moved
        new_global[:, cols] = glob[:, cols] - outer_rate * (delta + nesterov * moved)

    seven_l(0, 3, l_s)
    seven_l(3, 1, l_s)


def store(params, tok, glob, mom, params_out, tokens_out, glob_out, mom_out, sems):
    core = lax.rem(lax.axis_index("replica"), 2)
    copies = [
        pltpu.make_async_copy(
            tok.at[:, pl.ds(place, width)], tokens_out.at[:, pl.ds(start, width)], sems.at[i]
        )
        for i, (start, place, width) in enumerate(pieces(core))
    ]
    n = len(copies)
    for i, (src, dst) in enumerate(((params, params_out), (glob, glob_out), (mom, mom_out))):
        copies.append(pltpu.make_async_copy(src, dst, sems.at[n + i]))
    for cp in copies:
        cp.start()
    for cp in copies:
        cp.wait()


def shards(params, tokens, cotangent, gain, glob, momentum, prev_global):
    vmem = pl.BlockSpec(memory_space=pltpu.VMEM)
    hbm = pl.BlockSpec(memory_space=pl.ANY)
    dma = pltpu.SemaphoreType.DMA
    out = pl.pallas_call(
        kernel,
        out_shape=(
            pltpu.VMEM((S, HV), BF16),
            pltpu.VMEM((T, D), BF16),
            pltpu.VMEM((OWN, HV), F32),
            pltpu.VMEM((OWN, HV), F32),
        ),
        in_specs=[hbm, hbm, hbm, hbm, vmem, vmem, vmem],
        out_specs=(vmem, vmem, vmem, vmem),
        scratch_shapes=[
            pltpu.VMEM((2 * T, HV), BF16),
            pltpu.VMEM((T, 128), F32),
            pltpu.VMEM((1, D), F32),
            pltpu.VMEM((1, D), F32),
            pltpu.VMEM((2, Q, T), BF16),
            pltpu.VMEM((2, Q, 2 * T), BF16),
            pltpu.VMEM((2, Q + 64, HV), BF16),
            pltpu.VMEM((2, NC, S, CW), BF16),
            pltpu.VMEM((2, NC, S, CW), BF16),
            pltpu.VMEM((2, NC, S, CW), F32),
            pltpu.VMEM((NC, S, CW), BF16),
            pltpu.VMEM((NC, S, CW), BF16),
            pltpu.VMEM((2 * NC, S, 128), BF16),
            pltpu.VMEM((NC, 8, YR, 128), BF16),
            pltpu.VMEM((NC, YR, 128), F32),
            pltpu.VMEM((NC, 8, WR, 128), F32),
            pltpu.VMEM((2 * NC, WR, 128), F32),
            pltpu.VMEM((T, 2 * Q), BF16),
            pltpu.VMEM((T, D), BF16),
            pltpu.VMEM((OWN, HV), F32),
            pltpu.VMEM((PZ, HV // 2), F32),
            pltpu.VMEM((2, 2, PZ, HV // 2), BF16),
            pltpu.VMEM((YR, HV // 2), F32),
            pltpu.VMEM((2, S, HV // 2), BF16),
            dma((6 + NT,)), dma((6 + NT,)),
            dma((5 + 2 * NC,)), dma((5 + 2 * NC,)),
            dma((NZ + NC + 1,)), dma((NZ + NC + 1,)),
            dma((2,)), dma((2,)),
            dma((3 + NC,)), dma((3 + NC,)),
            dma((5,)), dma((5,)),
            dma((10,)),
        ],
        compiler_params=pltpu.CompilerParams(
            collective_id=0, has_side_effects=True, vmem_limit_bytes=54 * 1024 * 1024
        ),
        cost_estimate=pl.CostEstimate(
            flops=4 * T * D * HV, bytes_accessed=16 * 1024 * 1024, transcendentals=T
        ),
        name="diloco",
    )(params[0], tokens[0], cotangent[0], gain, glob, momentum, prev_global)
    out = pl.pallas_call(
        store,
        out_shape=tuple(jax.ShapeDtypeStruct(v.shape, v.dtype) for v in out),
        in_specs=[vmem] * len(out),
        out_specs=[hbm] * len(out),
        scratch_shapes=[dma((9,))],
        compiler_params=pltpu.CompilerParams(vmem_limit_bytes=1024 * 1024),
        name="store",
    )(*out)
    return (out[0][None], out[1][None], out[2], out[3])


def solution(mesh):
    placed = (
        P("replica", "fsdp", None),
        P("replica", "fsdp", None),
        P("replica", "fsdp", None),
        P(),
        P(("fsdp", "replica"), None),
        P(("fsdp", "replica"), None),
        P(("fsdp", "replica"), None),
    )
    return jax.shard_map(
        shards,
        mesh=mesh,
        in_specs=placed,
        out_specs=(
            P("replica", "fsdp", None),
            P("replica", "fsdp", None),
            P(("fsdp", "replica"), None),
            P(("fsdp", "replica"), None),
        ),
        check_vma=False,
    )
```
